32 devices in a mesh: seq: 8 (over z, y), head: 4 (over x, core).
Axes of the slice: x: 2, y: 2, z: 4, core: 2. Of those that a mesh axis runs over, the one named last changes fastest.
Arguments:
- queries: bfloat16 [1024, 16, 128], P('seq', 'head'), may hold values from -6 to 6
- keys: bfloat16 [1024, 2, 16, 128], P('seq', None, 'head'), may hold values from -6 to 6
- values: bfloat16 [1024, 2, 16, 128], P('seq', None, 'head'), may hold values from -6 to 6
- betas: float32 [1024, 2, 16], P('seq', None, 'head'), may hold values from 0.5 to 2, as said below
- gain: float32 [128], replicated, may hold values from 0.1 to 1.9
- out_grad: bfloat16 [1024, 16, 128], P('seq', 'head'), may hold values from -6 to 6
Outputs:
- normed_out: bfloat16 [1024, 16, 128], P('seq', 'head')
- query_grad: bfloat16 [1024, 16, 128], P('seq', 'head')
- key_grad: bfloat16 [1024, 2, 16, 128], P('seq', None, 'head')
- value_grad: bfloat16 [1024, 2, 16, 128], P('seq', None, 'head')
- beta_grad: float32 [1024, 2, 16], P('seq', None, 'head')
- gain_grad: float32 [128], replicated
The draws below stay inside these ranges and needn't reach their ends.
Inputs may be any that keep to these rules, and one draw needn't show every extreme that they name: `betas`: every step size lies strictly between 0 and 2.
All inputs are finite; a program needn't handle non-finite values.
Results may differ from the reference program's by a relative error of at most 0.003.
Values sent between devices are 32-bit elements; how exact they have to be, the bound alone decides.
No kernel may reach another device: no remote copies, remote signals or barrier semaphores. Data moves between devices by JAX's collectives and lax.ppermute only.
A program may use at most 128 MiB of HBM per device.

```python
import math
import jax
import jax.numpy as jnp
from jax import lax

HEADS = 16
DK = 128
DV = 128
STEPS = 2
TOKENS = 1024


def draw_betas(key, part):
    key_slow, key_rate, key_jitter, key_fast = jax.random.split(key, 4)
    slow_share = 0.5
    slow_heads = jax.random.uniform(key_slow, (HEADS,), jnp.float32) < slow_share
    slow_rates = jnp.exp(jax.random.uniform(key_rate, (HEADS,), jnp.float32, minval=math.log(0.05), maxval=0.0))
    jitter = jax.random.uniform(key_jitter, (TOKENS, STEPS, HEADS), jnp.float32, minval=0.5, maxval=1.5)
    slow_beta = 2.0 - slow_rates * jitter * (DK / (2.0 * TOKENS))
    fast_beta = jax.random.uniform(key_fast, (TOKENS, STEPS, HEADS), jnp.float32, minval=0.5, maxval=1.5)
    return jnp.where(slow_heads, slow_beta, fast_beta).astype(jnp.float32)


def shard_levels(own_key, shape, cuts, least, largest):
    def one(position, blocks):
        draws = jax.random.uniform(jax.random.fold_in(jax.random.fold_in(own_key, 6), position), (blocks,), jnp.float32, least / len(cuts), largest / len(cuts))
        return jnp.repeat(jnp.exp(draws), shape[position] // blocks).reshape((-1,) + (1,) * (len(shape) - position - 1))

    level = one(*cuts[0])
    for cut in cuts[1:]:
        level = level * one(*cut)
    return level


def gaussian(own_key, shape, deviation, reach, shards=(), held_as=jnp.bfloat16):
    result = jax.random.normal(own_key, shape, jnp.float32) * deviation
    if len(shards) > 0:
        result = shard_levels(own_key, shape, shards, -0.22, 0.18) * result
    return jnp.clip(result, min=-reach, max=reach).astype(held_as)


def setup_inputs(seed: int = 0) -> dict:
    arg_keys = jax.random.split(jax.random.key(seed), 7)
    queries = gaussian(arg_keys[0], (TOKENS, HEADS, DK), 1.0, 6.0, ((0, 8), (1, 4)))
    keys = gaussian(arg_keys[1], (TOKENS, STEPS, HEADS, DK), 1.0, 6.0, ((0, 8), (2, 4)))
    values = gaussian(arg_keys[2], (TOKENS, STEPS, HEADS, DV), 1.0, 6.0, ((0, 8), (2, 4)))
    betas = draw_betas(jax.random.fold_in(arg_keys[6], 71), 0)
    gain = jnp.clip(1.0 + 0.18 * jax.random.normal(arg_keys[4], (DV,), jnp.float32), 0.1, 1.9)
    out_grad = gaussian(arg_keys[5], (TOKENS, HEADS, DV), 1.0, 6.0, ((0, 8), (1, 4)))
    return {"queries": queries, "keys": keys, "values": values, "betas": betas, "gain": gain, "out_grad": out_grad}


EPS = 1e-06
HIGH_ACCURACY = lax.Precision.HIGHEST

def unit_rows(vectors):
    return vectors * lax.rsqrt(lax.optimization_barrier(jnp.sum(vectors * vectors, axis=-1, keepdims=True)) + EPS)

def recurrence(queries, keys, values, betas, gain):
    q_unit = unit_rows(queries)
    k_unit = unit_rows(keys)
    length = q_unit.shape[0]
    block_len = math.gcd(128, length)
    block_count = length // block_len
    q_blocks = q_unit.reshape(block_count, block_len, HEADS, DK)
    k_blocks = k_unit.reshape(block_count, block_len, STEPS, HEADS, DK)
    v_blocks = values.reshape(block_count, block_len, STEPS, HEADS, DV)
    b_blocks = betas.reshape(block_count, block_len, STEPS, HEADS)

    def token_step(memory_matrix, token_items):
        current_query, current_key, current_value, beta_now = token_items
        for reflection_step in range(STEPS):
            error_vector = current_value[reflection_step] - jnp.einsum('rdf,rd->rf', memory_matrix, current_key[reflection_step], precision=HIGH_ACCURACY)
            memory_matrix = memory_matrix + beta_now[reflection_step][:, None, None] * current_key[reflection_step][:, :, None] * error_vector[:, None, :]
        state_readout = jnp.einsum('rdf,rd->rf', memory_matrix, current_query, precision=HIGH_ACCURACY)
        return (memory_matrix, state_readout)

    def block_step(memory_matrix, block_items):
        return lax.scan(token_step, memory_matrix, block_items)
    block_step = jax.checkpoint(block_step)
    initial = jnp.zeros((HEADS, DK, DV), jnp.float32)
    _, readouts = lax.scan(block_step, initial, (q_blocks, k_blocks, v_blocks, b_blocks))
    readouts = readouts.reshape(length, HEADS, DV)
    inv_rms = lax.rsqrt(lax.optimization_barrier(jnp.mean(readouts * readouts, axis=-1, keepdims=True)) + EPS)
    return gain * (readouts * inv_rms)

def reference(queries, keys, values, betas, gain, out_grad):
    inputs = (queries.astype(jnp.float32), keys.astype(jnp.float32), values.astype(jnp.float32), betas, gain)
    normed, pullback = jax.vjp(recurrence, *inputs)
    gradients = pullback(out_grad.astype(jnp.float32))
    return (normed.astype(jnp.bfloat16), gradients[0].astype(jnp.bfloat16), gradients[1].astype(jnp.bfloat16), gradients[2].astype(jnp.bfloat16), gradients[3], gradients[4])
```

```python
import functools

import jax
import jax.numpy as jnp
from jax import lax
from jax.experimental import pallas as pl
from jax.experimental.pallas import tpu as pltpu
from jax.sharding import PartitionSpec as P

EPS = 1e-06
GROUP = 4
HALF = 128
BASE = 16
F32 = jnp.float32
BF16 = jnp.bfloat16


def mm(a, b, ta=False, tb=False):
    dims = (((0 if ta else 1,), (1 if tb else 0,)), ((), ()))
    return lax.dot_general(
        a, b, dims, precision=lax.Precision.HIGH, preferred_element_type=F32
    )


def exact_nt(a, b):
    return lax.dot_general(a, b, (((1,), (1,)), ((), ())), preferred_element_type=F32)


def iota(shape, dim):
    return lax.broadcasted_iota(jnp.int32, shape, dim)


def row_of(column):
    square = jnp.where(iota((HALF, HALF), 0) == iota((HALF, HALF), 1), column, 0.0)
    return jnp.sum(square, axis=0, keepdims=True)


def rate_column(rates, head):
    return jnp.sum(jnp.where(iota(rates.shape, 1) == head, rates, 0.0), axis=1, keepdims=True)


def small_inverses(lower, rate_row):
    blocks = HALF // BASE
    lane = iota((BASE, HALF), 1)
    row = iota((BASE, HALF), 0)
    packed = jnp.zeros((BASE, HALF), F32)
    for b in range(blocks):
        packed = jnp.where(lane // BASE == b, lower[b * BASE : (b + 1) * BASE], packed)
    scaled = packed * rate_row
    for j in range(BASE - 1):
        index = lane // BASE * BASE + j
        factor = jnp.take_along_axis(scaled, index, axis=1, mode="promise_in_bounds")
        packed = packed - jnp.where(row > j, factor, 0.0) * packed[j : j + 1]
    return jnp.concatenate(
        [jnp.where(lane // BASE == b, packed, 0.0) for b in range(blocks)], axis=0
    )


def first_kernel(
    group, k_ref, v_ref, rates_ref, ts0, ts1, ts2, ts3, ku_ref, n_ref, w_ref, e_ref, kf, vf
):
    me = lax.rem(lax.axis_index("seq"), group)
    kf[...] = k_ref[...].astype(F32)
    vf[...] = v_ref[...].astype(F32)
    heads = range(len((ts0, ts1, ts2, ts3)))
    steps = rates_ref.shape[0]
    stride = kf.shape[0] // steps
    rates = rates_ref[...]
    strict = iota((HALF, HALF), 1) < iota((HALF, HALF), 0)
    unit, vals, rate, rate_rows, diag, cross = [], [], [], [], [], []
    for i in heads:
        head = me ^ i
        raw = kf[pl.ds(head, steps, stride=stride), :]
        inv = lax.rsqrt(jnp.sum(raw * raw, axis=1, keepdims=True) + EPS)
        column = rate_column(rates, head)
        unit.append(raw * inv)
        ku_ref[i] = unit[i]
        vals.append(vf[pl.ds(head, steps, stride=stride), :])
        rate.append(column)
        rate_rows.append([row_of(column[:HALF]), row_of(column[HALF:])])
        inv_rows = [row_of(inv[:HALF]), row_of(inv[HALF:])]
        raw16 = raw.astype(BF16)
        halves = [raw16[:HALF], raw16[HALF:]]
        diag.append(
            [
                jnp.where(
                    strict,
                    exact_nt(halves[b], halves[b])
                    * inv[b * HALF : (b + 1) * HALF]
                    * inv_rows[b],
                    0.0,
                )
                for b in range(2)
            ]
        )
        cross.append(exact_nt(halves[1], halves[0]) * inv[HALF:] * inv_rows[0])
    jobs = [(i, b) for i in heads for b in range(2)]
    inverse = {job: small_inverses(diag[job[0]][job[1]], rate_rows[job[0]][job[1]]) for job in jobs}
    size = BASE
    while size < HALF:
        r, c = iota((HALF, HALF), 0) // size, iota((HALF, HALF), 1) // size
        below = (r % 2 == 1) & (c == r - 1)
        part = {(i, b): jnp.where(below, diag[i][b], 0.0) for i, b in jobs}
        right = {
            (i, b): part[i, b] - mm(part[i, b] * rate_rows[i][b], inverse[i, b]) for i, b in jobs
        }
        inverse = {
            (i, b): inverse[i, b]
            + right[i, b]
            - mm(inverse[i, b] * rate_rows[i][b], right[i, b])
            for i, b in jobs
        }
        size *= 2
    right = [cross[i] - mm(cross[i] * rate_rows[i][0], inverse[i, 0]) for i in heads]
    joined = [right[i] - mm(inverse[i, 1] * rate_rows[i][1], right[i]) for i in heads]
    solved = []
    for i in heads:
        n_ref[i, :HALF, :HALF] = inverse[i, 0]
        n_ref[i, :HALF, HALF:] = jnp.zeros((HALF, HALF), F32)
        n_ref[i, HALF:, :HALF] = joined[i]
        n_ref[i, HALF:, HALF:] = inverse[i, 1]
        both = jnp.concatenate([unit[i], vals[i]], axis=1)
        top = both[:HALF] - mm(inverse[i, 0] * rate_rows[i][0], both[:HALF])
        low = jnp.concatenate(
            [joined[i] * rate_rows[i][0], inverse[i, 1] * rate_rows[i][1]], axis=1
        )
        bottom = both[HALF:] - mm(low, both)
        solved.append(jnp.concatenate([top, bottom], axis=0))
    eye = (iota((HALF, 2 * HALF), 0) == iota((HALF, 2 * HALF), 1)).astype(F32)
    sign = jnp.where(iota((HALF, 2 * HALF), 1) < HALF, -1.0, 1.0)
    for i, ts in zip(heads, (ts0, ts1, ts2, ts3)):
        w_ref[i] = solved[i][:, :HALF]
        e_ref[i] = solved[i][:, HALF:]
        ts[...] = eye + sign * mm(unit[i], rate[i] * solved[i], ta=True)


def second_kernel(
    group, q_ref, rates_ref, ku_ref, n_ref, w_ref, e_ref, qu_ref, s_ref, qc_ref, o_ref, kx_ref, qf
):
    me = lax.rem(lax.axis_index("seq"), group)
    qf[...] = q_ref[...].astype(F32)
    heads, steps = ku_ref.shape[:2]
    tokens = steps // 2
    stride = qf.shape[0] // tokens
    rates = rates_ref[...]
    seen = iota((tokens, steps), 1) <= 2 * iota((tokens, steps), 0) + 1
    for i in range(heads):
        head = me ^ i
        raw = qf[pl.ds(head, tokens, stride=stride), :]
        unit = raw * lax.rsqrt(jnp.sum(raw * raw, axis=1, keepdims=True) + EPS)
        qu_ref[i] = unit
        rate = rate_column(rates, head)
        scores = jnp.where(seen, mm(unit, ku_ref[i], tb=True), 0.0)
        s_ref[i] = scores
        weighted = rate * jnp.concatenate([w_ref[i], e_ref[i]], axis=1)
        seen_rows = mm(scores, weighted)
        qc_ref[i] = unit - seen_rows[:, :HALF]
        o_ref[i] = seen_rows[:, HALF:]
        kx_ref[i] = ku_ref[i] - mm(n_ref[i], rate * ku_ref[i], ta=True)


def join_kernel(group, p0, p1, p2, p3, starts_ref, total_ref, maps_ref):
    me = lax.rem(lax.axis_index("seq"), group)
    for i, piece in enumerate((p0, p1, p2, p3)):
        maps_ref[me ^ i] = piece[...]
    state = jnp.zeros((HALF, HALF), F32)
    for j in range(group):
        starts_ref[j] = state
        own = maps_ref[j, :, HALF:]
        state = own if j == 0 else mm(maps_ref[j, :, :HALF], state) + own
    total_ref[...] = state


def products_kernel(group, maps_ref, before_ref, after_ref):
    eye = (iota((HALF, HALF), 0) == iota((HALF, HALF), 1)).astype(F32)
    before, after = None, None
    for j in range(group + 1):
        before_ref[j] = eye if before is None else before
        if j < group:
            step = maps_ref[j, :, :HALF]
            before = step if before is None else mm(step, before)
    for j in reversed(range(group)):
        after_ref[j] = eye if after is None else after
        step = maps_ref[j, :, :HALF]
        after = step if after is None else mm(after, step)


def spread_kernel(group, transposed, entry_ref, starts_ref, maps_ref, o0, o1, o2, o3):
    me = lax.rem(lax.axis_index("seq"), group)
    entry = entry_ref[...]
    for i, out in enumerate((o0, o1, o2, o3)):
        out[...] = starts_ref[me ^ i] + mm(maps_ref[me ^ i], entry, ta=transposed)


def read_kernel(
    group,
    s0,
    s1,
    s2,
    s3,
    og_ref,
    gain_ref,
    qc_ref,
    o_ref,
    w_ref,
    e_ref,
    p0,
    p1,
    p2,
    p3,
    out_ref,
    grad_ref,
    err_ref,
    gf,
    of,
):
    me = lax.rem(lax.axis_index("seq"), group)
    gf[...] = og_ref[...].astype(F32)
    tokens = qc_ref.shape[1]
    stride = gf.shape[0] // tokens
    gain = gain_ref[...]
    gain_part = jnp.zeros((1, HALF), F32)
    for i, (state_ref, part) in enumerate(zip((s0, s1, s2, s3), (p0, p1, p2, p3))):
        head = me ^ i
        state = state_ref[...]
        read = o_ref[i] + mm(qc_ref[i], state)
        inv_rms = lax.rsqrt(jnp.mean(read * read, axis=1, keepdims=True) + EPS)
        normal = read * inv_rms
        of[pl.ds(head, tokens, stride=stride), :] = gain * normal
        given = gf[pl.ds(head, tokens, stride=stride), :]
        gain_part = gain_part + jnp.sum(given * normal, axis=0, keepdims=True)
        scaled = given * gain
        grad = inv_rms * (scaled - normal * jnp.mean(scaled * normal, axis=1, keepdims=True))
        grad_ref[i] = grad
        part[:HALF, :] = mm(qc_ref[i], grad, ta=True)
        err_ref[i] = e_ref[i] - mm(w_ref[i], state)
    for part in (p0, p1, p2, p3):
        part[HALF:, :] = jnp.broadcast_to(gain_part, (8, HALF))
    out_ref[...] = of[...].astype(BF16)


def early_kernel(
    group,
    s0,
    s1,
    s2,
    s3,
    q_ref,
    rates_ref,
    grad_ref,
    err_ref,
    qu_ref,
    ku_ref,
    sc_ref,
    n_ref,
    dq_ref,
    dk_ref,
    z_ref,
    qf,
    df,
):
    me = lax.rem(lax.axis_index("seq"), group)
    qf[...] = q_ref[...].astype(F32)
    heads, steps = ku_ref.shape[:2]
    tokens = steps // 2
    stride = qf.shape[0] // tokens
    rates = rates_ref[...]
    seen = iota((tokens, steps), 1) <= 2 * iota((tokens, steps), 0) + 1
    for i, state_ref in enumerate((s0, s1, s2, s3)):
        head = me ^ i
        rate = rate_column(rates, head)
        grad = grad_ref[i]
        unit = qu_ref[i]
        d_scores = jnp.where(seen, mm(grad, rate * err_ref[i], tb=True), 0.0)
        d_unit = mm(grad, state_ref[...], tb=True) + mm(d_scores, ku_ref[i])
        raw = qf[pl.ds(head, tokens, stride=stride), :]
        inv = lax.rsqrt(jnp.sum(raw * raw, axis=1, keepdims=True) + EPS)
        df[pl.ds(head, tokens, stride=stride), :] = inv * (
            d_unit - unit * jnp.sum(unit * d_unit, axis=1, keepdims=True)
        )
        dk_ref[i] = mm(d_scores, unit, ta=True)
        d_pseudo = mm(sc_ref[i], grad, ta=True)
        z_ref[i] = d_pseudo - mm(n_ref[i], rate * d_pseudo, ta=True)
    dq_ref[...] = df[...].astype(BF16)


def join_back_kernel(group, p0, p1, p2, p3, maps_ref, starts_ref, total_ref, parts):
    me = lax.rem(lax.axis_index("seq"), group)
    gain = jnp.zeros((8, HALF), F32)
    for i, piece in enumerate((p0, p1, p2, p3)):
        parts[me ^ i] = piece[:HALF, :]
        gain = gain + piece[HALF:, :]
    adjoint = jnp.zeros((HALF, HALF), F32)
    for j in reversed(range(group)):
        starts_ref[j] = adjoint
        own = parts[j]
        adjoint = own if j == group - 1 else mm(maps_ref[j, :, :HALF], adjoint, ta=True) + own
    total_ref[:HALF, :] = adjoint
    total_ref[HALF:, :] = gain


def last_kernel(
    group,
    a0,
    a1,
    a2,
    a3,
    s0,
    s1,
    s2,
    s3,
    k_ref,
    rates_ref,
    ku_ref,
    kx_ref,
    err_ref,
    z_ref,
    dk0_ref,
    dk_ref,
    dv_ref,
    db_ref,
    kf,
    df,
    vf,
):
    me = lax.rem(lax.axis_index("seq"), group)
    kf[...] = k_ref[...].astype(F32)
    heads, steps = ku_ref.shape[:2]
    stride = kf.shape[0] // steps
    rates = rates_ref[...]
    strict = iota((steps, steps), 1) < iota((steps, steps), 0)
    d_rates = jnp.zeros(rates.shape, F32)
    for i, (adjoint_ref, state_ref) in enumerate(zip((a0, a1, a2, a3), (s0, s1, s2, s3))):
        head = me ^ i
        adjoint, state = adjoint_ref[...], state_ref[...]
        rate = rate_column(rates, head)
        unit, err = ku_ref[i], err_ref[i]
        pseudo = rate * err
        z = z_ref[i] + mm(kx_ref[i], adjoint)
        d_value = rate * z
        d_rate = jnp.sum(z * err, axis=1, keepdims=True)
        d_rates = jnp.where(iota(rates.shape, 1) == head, d_rate, d_rates)
        vf[pl.ds(head, steps, stride=stride), :] = d_value
        d_lower = jnp.where(strict, mm(d_value, pseudo, tb=True), 0.0)
        d_unit = dk0_ref[i] + mm(pseudo, adjoint, tb=True) - mm(d_value, state, tb=True)
        d_unit = d_unit - mm(d_lower, unit) - mm(d_lower, unit, ta=True)
        raw = kf[pl.ds(head, steps, stride=stride), :]
        inv = lax.rsqrt(jnp.sum(raw * raw, axis=1, keepdims=True) + EPS)
        df[pl.ds(head, steps, stride=stride), :] = inv * (
            d_unit - unit * jnp.sum(unit * d_unit, axis=1, keepdims=True)
        )
    dk_ref[...] = df[...].astype(BF16)
    dv_ref[...] = vf[...].astype(BF16)
    db_ref[...] = d_rates


def f32(*shape):
    return jax.ShapeDtypeStruct(shape, F32)


def b16(*shape):
    return jax.ShapeDtypeStruct(shape, BF16)


def call(body, outs, *args, scratch=()):
    return pl.pallas_call(
        body,
        out_shape=outs,
        scratch_shapes=[pltpu.VMEM(s, F32) for s in scratch],
        compiler_params=pltpu.CompilerParams(vmem_limit_bytes=56 * 1024 * 1024),
    )(*args)


def swapped(pieces, group):
    count = lax.axis_size("seq")
    return [
        piece if i == 0 else lax.ppermute(piece, "seq", [(d, d ^ i) for d in range(count)])
        for i, piece in enumerate(pieces)
    ]


def local(queries, keys, values, betas, gain, out_grad):
    tokens, heads, dim = queries.shape
    substeps = keys.shape[1]
    steps = tokens * substeps
    group = GROUP
    count = lax.axis_size("seq")
    groups = count // group
    bind = functools.partial
    q2 = queries.reshape(tokens * heads, dim)
    g2 = out_grad.reshape(tokens * heads, dim)
    k2 = keys.reshape(steps * heads, dim)
    v2 = values.reshape(steps * heads, dim)
    rates = betas.reshape(steps, heads)
    gain2 = gain.reshape(1, dim)

    *maps, ku, inverse, w, e = call(
        bind(first_kernel, group),
        [f32(dim, 2 * dim)] * heads
        + [
            f32(heads, steps, dim),
            f32(heads, steps, steps),
            f32(heads, steps, dim),
            f32(heads, steps, dim),
        ],
        k2,
        v2,
        rates,
        scratch=[(steps * heads, dim)] * 2,
    )
    got = swapped(maps, group)
    qu, scores, qc, o_part, kx = call(
        bind(second_kernel, group),
        [
            f32(heads, tokens, dim),
            f32(heads, tokens, steps),
            f32(heads, tokens, dim),
            f32(heads, tokens, dim),
            f32(heads, steps, dim),
        ],
        q2,
        rates,
        ku,
        inverse,
        w,
        e,
        scratch=[(tokens * heads, dim)],
    )
    starts, total, by_place = call(
        bind(join_kernel, group),
        [f32(group, dim, dim), f32(dim, dim), f32(group, dim, 2 * dim)],
        *got,
    )
    ahead = [(d, d + group) for d in range(count - group)]
    behind = [(d + group, d) for d in range(count - group)]
    entry = lax.ppermute(total, "seq", ahead)
    before, after = call(
        bind(products_kernel, group), [f32(group + 1, dim, dim), f32(group, dim, dim)], by_place
    )
    for _ in range(groups - 2):
        passed = jnp.dot(before[group], entry, precision=lax.Precision.HIGHEST) + total
        entry = lax.ppermute(passed, "seq", ahead)
    states = call(
        bind(spread_kernel, group, False), [f32(dim, dim)] * heads, entry, starts, before
    )
    states = swapped(states, group)
    *parts, normed, o_grad, err = call(
        bind(read_kernel, group),
        [f32(dim + 8, dim)] * heads
        + [b16(tokens * heads, dim), f32(heads, tokens, dim), f32(heads, steps, dim)],
        *states,
        g2,
        gain2,
        qc,
        o_part,
        w,
        e,
        scratch=[(tokens * heads, dim)] * 2,
    )
    got_parts = swapped(parts, group)
    dq, dk0, z0 = call(
        bind(early_kernel, group),
        [b16(tokens * heads, dim), f32(heads, steps, dim), f32(heads, steps, dim)],
        *states,
        q2,
        rates,
        o_grad,
        err,
        qu,
        ku,
        scores,
        inverse,
        scratch=[(tokens * heads, dim)] * 2,
    )
    starts, total = call(
        bind(join_back_kernel, group),
        [f32(group, dim, dim), f32(dim + 8, dim)],
        *got_parts,
        by_place,
        scratch=[(group, dim, dim)],
    )
    if groups == 2:
        other = lax.ppermute(total, "seq", [(d, d ^ group) for d in range(count)])
        here = lax.axis_index("seq") < group
        entry = jnp.where(here, other[:dim], 0.0)
        gain_sum = total[dim] + other[dim]
        head_count = lax.axis_size("head")
        hops = 1
        while hops < head_count:
            gain_sum = gain_sum + lax.ppermute(
                gain_sum, "head", [(d, d ^ hops) for d in range(head_count)]
            )
            hops *= 2
    else:
        entry = lax.ppermute(total[:dim], "seq", behind)
        gain_sum = lax.psum(parts[0][dim], ("seq", "head"))
    for _ in range(groups - 2):
        passed = (
            jnp.dot(before[group].T, entry, precision=lax.Precision.HIGHEST) + total[:dim]
        )
        entry = lax.ppermute(passed, "seq", behind)
    adjoints = call(
        bind(spread_kernel, group, True), [f32(dim, dim)] * heads, entry, starts, after
    )
    adjoints = swapped(adjoints, group)
    dk, dv, db = call(
        bind(last_kernel, group),
        [b16(steps * heads, dim), b16(steps * heads, dim), f32(steps, heads)],
        *adjoints,
        *states,
        k2,
        rates,
        ku,
        kx,
        err,
        z0,
        dk0,
        scratch=[(steps * heads, dim)] * 3,
    )
    return (
        normed.reshape(tokens, heads, dim),
        dq.reshape(tokens, heads, dim),
        dk.reshape(tokens, substeps, heads, dim),
        dv.reshape(tokens, substeps, heads, dim),
        db.reshape(tokens, substeps, heads),
        gain_sum,
    )


def solution(mesh):
    return jax.shard_map(
        local,
        mesh=mesh,
        in_specs=(
            P("seq", "head", None),
            P("seq", None, "head", None),
            P("seq", None, "head", None),
            P("seq", None, "head"),
            P(),
            P("seq", "head", None),
        ),
        out_specs=(
            P("seq", "head", None),
            P("seq", "head", None),
            P("seq", None, "head", None),
            P("seq", None, "head", None),
            P("seq", None, "head"),
            P(),
        ),
        check_vma=False,
    )
```

```python
import functools

import jax
import jax.numpy as jnp
from jax import lax
from jax.experimental import pallas as pl
from jax.experimental.pallas import tpu as pltpu
from jax.sharding import PartitionSpec as P

EPS = 1e-06
GROUP = 4
HALF = 128
BASE = 16
F32 = jnp.float32
BF16 = jnp.bfloat16


def mm(a, b, ta=False, tb=False):
    dims = (((0 if ta else 1,), (1 if tb else 0,)), ((), ()))
    return lax.dot_general(
        a, b, dims, precision=lax.Precision.HIGH, preferred_element_type=F32
    )


def exact_nt(a, b):
    return lax.dot_general(a, b, (((1,), (1,)), ((), ())), preferred_element_type=F32)


def iota(shape, dim):
    return lax.broadcasted_iota(jnp.int32, shape, dim)


def row_of(column):
    square = jnp.where(iota((HALF, HALF), 0) == iota((HALF, HALF), 1), column, 0.0)
    return jnp.sum(square, axis=0, keepdims=True)


def places(steps, j):
    shape = (steps, steps // 2)
    return (iota(shape, 0) == 2 * iota(shape, 1) + j).astype(F32)


def pick(a, b, ta=False, tb=False):
    dims = (((0 if ta else 1,), (1 if tb else 0,)), ((), ()))
    return lax.dot_general(
        a, b, dims, precision=lax.Precision.HIGHEST, preferred_element_type=F32
    )


def rate_column(rates, head):
    return jnp.sum(jnp.where(iota(rates.shape, 1) == head, rates, 0.0), axis=1, keepdims=True)


def small_inverses(lower, rate_row):
    blocks = HALF // BASE
    lane = iota((BASE, HALF), 1)
    row = iota((BASE, HALF), 0)
    packed = jnp.zeros((BASE, HALF), F32)
    for b in range(blocks):
        packed = jnp.where(lane // BASE == b, lower[b * BASE : (b + 1) * BASE], packed)
    scaled = packed * rate_row
    for j in range(BASE - 1):
        index = lane // BASE * BASE + j
        factor = jnp.take_along_axis(scaled, index, axis=1, mode="promise_in_bounds")
        packed = packed - jnp.where(row > j, factor, 0.0) * packed[j : j + 1]
    return jnp.concatenate(
        [jnp.where(lane // BASE == b, packed, 0.0) for b in range(blocks)], axis=0
    )


def first_kernel(
    group,
    k_ref,
    v_ref,
    packed_ref,
    ts0,
    ts1,
    ts2,
    ts3,
    ku_ref,
    n_ref,
    w_ref,
    e_ref,
    rates_ref,
    k16,
    v16,
    kf,
    vf,
    rows,
    sems,
):
    copies = [
        pltpu.make_async_copy(k_ref, k16, sems.at[0]),
        pltpu.make_async_copy(v_ref, v16, sems.at[1]),
    ]
    for copy in copies:
        copy.start()
    me = lax.rem(lax.axis_index("seq"), group)
    heads = range(len((ts0, ts1, ts2, ts3)))
    steps = rates_ref.shape[0]
    stride = kf.shape[0] // steps
    packed = packed_ref[...]
    own, place = [packed[: len(heads)], packed[len(heads) :]], [places(steps, j) for j in range(2)]
    rates = pick(place[0], own[0], tb=True) + pick(place[1], own[1], tb=True)
    rates_ref[...] = rates
    rows[...] = pick(own[0], place[0], tb=True) + pick(own[1], place[1], tb=True)
    strict = iota((HALF, HALF), 1) < iota((HALF, HALF), 0)
    unit, vals, rate, rate_rows, diag, cross = [], [], [], [], [], []
    copies[0].wait()
    kf[...] = k16[...].astype(F32)
    for i in heads:
        head = me ^ i
        raw = kf[pl.ds(head, steps, stride=stride), :]
        inv = lax.rsqrt(jnp.sum(raw * raw, axis=1, keepdims=True) + EPS)
        unit.append(raw * inv)
        ku_ref[i] = unit[i]
        rate.append(rate_column(rates, head))
        rate_row = rows[pl.ds(head, 1), :]
        rate_rows.append([rate_row[:, :HALF], rate_row[:, HALF:]])
        inv_rows = [row_of(inv[:HALF]), row_of(inv[HALF:])]
        raw16 = raw.astype(BF16)
        halves = [raw16[:HALF], raw16[HALF:]]
        diag.append(
            [
                jnp.where(
                    strict,
                    exact_nt(halves[b], halves[b])
                    * inv[b * HALF : (b + 1) * HALF]
                    * inv_rows[b],
                    0.0,
                )
                for b in range(2)
            ]
        )
        cross.append(exact_nt(halves[1], halves[0]) * inv[HALF:] * inv_rows[0])
    jobs = [(i, b) for i in heads for b in range(2)]
    inverse = {job: small_inverses(diag[job[0]][job[1]], rate_rows[job[0]][job[1]]) for job in jobs}
    size = BASE
    while size < HALF:
        r, c = iota((HALF, HALF), 0) // size, iota((HALF, HALF), 1) // size
        below = (r % 2 == 1) & (c == r - 1)
        part = {(i, b): jnp.where(below, diag[i][b], 0.0) for i, b in jobs}
        right = {
            (i, b): part[i, b] - mm(part[i, b] * rate_rows[i][b], inverse[i, b]) for i, b in jobs
        }
        inverse = {
            (i, b): inverse[i, b]
            + right[i, b]
            - mm(inverse[i, b] * rate_rows[i][b], right[i, b])
            for i, b in jobs
        }
        size *= 2
    right = [cross[i] - mm(cross[i] * rate_rows[i][0], inverse[i, 0]) for i in heads]
    joined = [right[i] - mm(inverse[i, 1] * rate_rows[i][1], right[i]) for i in heads]
    solved = []
    copies[1].wait()
    vf[...] = v16[...].astype(F32)
    for i in heads:
        vals.append(vf[pl.ds(me ^ i, steps, stride=stride), :])
        n_ref[i, :HALF, :HALF] = inverse[i, 0]
        n_ref[i, :HALF, HALF:] = jnp.zeros((HALF, HALF), F32)
        n_ref[i, HALF:, :HALF] = joined[i]
        n_ref[i, HALF:, HALF:] = inverse[i, 1]
        both = jnp.concatenate([unit[i], vals[i]], axis=1)
        top = both[:HALF] - mm(inverse[i, 0] * rate_rows[i][0], both[:HALF])
        low = jnp.concatenate(
            [joined[i] * rate_rows[i][0], inverse[i, 1] * rate_rows[i][1]], axis=1
        )
        bottom = both[HALF:] - mm(low, both)
        solved.append(jnp.concatenate([top, bottom], axis=0))
    eye = (iota((HALF, 2 * HALF), 0) == iota((HALF, 2 * HALF), 1)).astype(F32)
    sign = jnp.where(iota((HALF, 2 * HALF), 1) < HALF, -1.0, 1.0)
    for i, ts in zip(heads, (ts0, ts1, ts2, ts3)):
        w_ref[i] = solved[i][:, :HALF]
        e_ref[i] = solved[i][:, HALF:]
        ts[...] = eye + sign * mm(unit[i], rate[i] * solved[i], ta=True)


def second_kernel(
    group, q_ref, rates_ref, ku_ref, n_ref, w_ref, e_ref, qu_ref, s_ref, qc_ref, o_ref, kx_ref, qf
):
    me = lax.rem(lax.axis_index("seq"), group)
    qf[...] = q_ref[...].astype(F32)
    heads, steps = ku_ref.shape[:2]
    tokens = steps // 2
    stride = qf.shape[0] // tokens
    rates = rates_ref[...]
    seen = iota((tokens, steps), 1) <= 2 * iota((tokens, steps), 0) + 1
    for i in range(heads):
        head = me ^ i
        raw = qf[pl.ds(head, tokens, stride=stride), :]
        unit = raw * lax.rsqrt(jnp.sum(raw * raw, axis=1, keepdims=True) + EPS)
        qu_ref[i] = unit
        rate = rate_column(rates, head)
        scores = jnp.where(seen, mm(unit, ku_ref[i], tb=True), 0.0)
        s_ref[i] = scores
        weighted = rate * jnp.concatenate([w_ref[i], e_ref[i]], axis=1)
        seen_rows = mm(scores, weighted)
        qc_ref[i] = unit - seen_rows[:, :HALF]
        o_ref[i] = seen_rows[:, HALF:]
        kx_ref[i] = ku_ref[i] - mm(n_ref[i], rate * ku_ref[i], ta=True)


def join_kernel(group, p0, p1, p2, p3, starts_ref, total_ref, maps_ref):
    me = lax.rem(lax.axis_index("seq"), group)
    for i, piece in enumerate((p0, p1, p2, p3)):
        maps_ref[me ^ i] = piece[...]
    state = jnp.zeros((HALF, HALF), F32)
    for j in range(group):
        starts_ref[j] = state
        own = maps_ref[j, :, HALF:]
        state = own if j == 0 else mm(maps_ref[j, :, :HALF], state) + own
    total_ref[...] = state


def products_kernel(group, maps_ref, before_ref, after_ref):
    eye = (iota((HALF, HALF), 0) == iota((HALF, HALF), 1)).astype(F32)
    before, after = None, None
    for j in range(group + 1):
        before_ref[j] = eye if before is None else before
        if j < group:
            step = maps_ref[j, :, :HALF]
            before = step if before is None else mm(step, before)
    for j in reversed(range(group)):
        after_ref[j] = eye if after is None else after
        step = maps_ref[j, :, :HALF]
        after = step if after is None else mm(after, step)


def spread_kernel(group, side, transposed, other_ref, starts_ref, maps_ref, *outs):
    me = lax.rem(lax.axis_index("seq"), group)
    entry = other_ref[:HALF, :]
    if side is not None:
        entry = jnp.where(lax.axis_index("seq") // group == side, entry, 0.0)
    for i, out in enumerate(outs):
        out[:HALF, :] = starts_ref[me ^ i] + mm(maps_ref[me ^ i], entry, ta=transposed)


def spread_back_kernel(group, side, other_ref, starts_ref, maps_ref, gain_ref, *outs):
    spread_kernel(group, side, True, other_ref, starts_ref, maps_ref, *outs)
    for out in outs:
        out[HALF:, :] = gain_ref[...] + other_ref[HALF:, :]


def read_kernel(
    group,
    s0,
    s1,
    s2,
    s3,
    og_ref,
    gain_ref,
    qc_ref,
    o_ref,
    w_ref,
    e_ref,
    p0,
    p1,
    p2,
    p3,
    out_ref,
    grad_ref,
    err_ref,
    gain_part_ref,
    gf,
    of,
):
    me = lax.rem(lax.axis_index("seq"), group)
    gf[...] = og_ref[...].astype(F32)
    tokens = qc_ref.shape[1]
    stride = gf.shape[0] // tokens
    gain = gain_ref[...]
    gain_part = jnp.zeros((1, HALF), F32)
    for i, (state_ref, part) in enumerate(zip((s0, s1, s2, s3), (p0, p1, p2, p3))):
        head = me ^ i
        state = state_ref[...]
        read = o_ref[i] + mm(qc_ref[i], state)
        inv_rms = lax.rsqrt(jnp.mean(read * read, axis=1, keepdims=True) + EPS)
        normal = read * inv_rms
        of[pl.ds(head, tokens, stride=stride), :] = gain * normal
        given = gf[pl.ds(head, tokens, stride=stride), :]
        gain_part = gain_part + jnp.sum(given * normal, axis=0, keepdims=True)
        scaled = given * gain
        grad = inv_rms * (scaled - normal * jnp.mean(scaled * normal, axis=1, keepdims=True))
        grad_ref[i] = grad
        part[...] = mm(qc_ref[i], grad, ta=True)
        err_ref[i] = e_ref[i] - mm(w_ref[i], state)
    gain_part_ref[...] = jnp.broadcast_to(gain_part, (8, HALF))
    out_ref[...] = of[...].astype(BF16)


def early_kernel(
    group,
    s0,
    s1,
    s2,
    s3,
    q_ref,
    rates_ref,
    grad_ref,
    err_ref,
    qu_ref,
    ku_ref,
    sc_ref,
    n_ref,
    dq_ref,
    dk_ref,
    z_ref,
    qf,
    df,
):
    me = lax.rem(lax.axis_index("seq"), group)
    qf[...] = q_ref[...].astype(F32)
    heads, steps = ku_ref.shape[:2]
    tokens = steps // 2
    stride = qf.shape[0] // tokens
    rates = rates_ref[...]
    seen = iota((tokens, steps), 1) <= 2 * iota((tokens, steps), 0) + 1
    for i, state_ref in enumerate((s0, s1, s2, s3)):
        head = me ^ i
        rate = rate_column(rates, head)
        grad = grad_ref[i]
        unit = qu_ref[i]
        d_scores = jnp.where(seen, mm(grad, rate * err_ref[i], tb=True), 0.0)
        d_unit = mm(grad, state_ref[...], tb=True) + mm(d_scores, ku_ref[i])
        raw = qf[pl.ds(head, tokens, stride=stride), :]
        inv = lax.rsqrt(jnp.sum(raw * raw, axis=1, keepdims=True) + EPS)
        df[pl.ds(head, tokens, stride=stride), :] = inv * (
            d_unit - unit * jnp.sum(unit * d_unit, axis=1, keepdims=True)
        )
        dk_ref[i] = mm(d_scores, unit, ta=True)
        d_pseudo = mm(sc_ref[i], grad, ta=True)
        z_ref[i] = d_pseudo - mm(n_ref[i], rate * d_pseudo, ta=True)
    dq_ref[...] = df[...].astype(BF16)


def join_back_kernel(group, p0, p1, p2, p3, maps_ref, gain_ref, starts_ref, total_ref, parts):
    me = lax.rem(lax.axis_index("seq"), group)
    for i, piece in enumerate((p0, p1, p2, p3)):
        parts[me ^ i] = piece[...]
    adjoint = jnp.zeros((HALF, HALF), F32)
    for j in reversed(range(group)):
        starts_ref[j] = adjoint
        own = parts[j]
        adjoint = own if j == group - 1 else mm(maps_ref[j, :, :HALF], adjoint, ta=True) + own
    total_ref[:HALF, :] = adjoint
    total_ref[HALF:, :] = gain_ref[...]


def last_kernel(
    group,
    a0,
    a1,
    a2,
    a3,
    s0,
    s1,
    s2,
    s3,
    k_ref,
    rates_ref,
    ku_ref,
    kx_ref,
    err_ref,
    z_ref,
    dk0_ref,
    dk_ref,
    dv_ref,
    db_ref,
    gain_ref,
    kf,
    df,
    vf,
):
    me = lax.rem(lax.axis_index("seq"), group)
    kf[...] = k_ref[...].astype(F32)
    heads, steps = ku_ref.shape[:2]
    stride = kf.shape[0] // steps
    rates = rates_ref[...]
    strict = iota((steps, steps), 1) < iota((steps, steps), 0)
    d_rates = jnp.zeros(rates.shape, F32)
    for i, (adjoint_ref, state_ref) in enumerate(zip((a0, a1, a2, a3), (s0, s1, s2, s3))):
        head = me ^ i
        adjoint, state = adjoint_ref[:HALF, :], state_ref[...]
        rate = rate_column(rates, head)
        unit, err = ku_ref[i], err_ref[i]
        pseudo = rate * err
        z = z_ref[i] + mm(kx_ref[i], adjoint)
        d_value = rate * z
        d_rate = jnp.sum(z * err, axis=1, keepdims=True)
        d_rates = jnp.where(iota(rates.shape, 1) == head, d_rate, d_rates)
        vf[pl.ds(head, steps, stride=stride), :] = d_value
        d_lower = jnp.where(strict, mm(d_value, pseudo, tb=True), 0.0)
        d_unit = dk0_ref[i] + mm(pseudo, adjoint, tb=True) - mm(d_value, state, tb=True)
        d_unit = d_unit - mm(d_lower, unit) - mm(d_lower, unit, ta=True)
        raw = kf[pl.ds(head, steps, stride=stride), :]
        inv = lax.rsqrt(jnp.sum(raw * raw, axis=1, keepdims=True) + EPS)
        df[pl.ds(head, steps, stride=stride), :] = inv * (
            d_unit - unit * jnp.sum(unit * d_unit, axis=1, keepdims=True)
        )
    dk_ref[...] = df[...].astype(BF16)
    dv_ref[...] = vf[...].astype(BF16)
    for j in range(2):
        db_ref[j * heads : (j + 1) * heads, :] = pick(d_rates, places(steps, j), ta=True)
    gain_ref[...] = a0[HALF:, :] + a1[HALF:, :] + a2[HALF:, :] + a3[HALF:, :]


def f32(*shape):
    return pltpu.VMEM(shape, F32)


def out(dtype, *shape):
    return jax.ShapeDtypeStruct(shape, dtype)


def call(body, outs, *args, scratch=(), specs=None):
    return pl.pallas_call(
        body,
        out_shape=outs,
        in_specs=specs or [pl.BlockSpec(memory_space=pltpu.VMEM)] * len(args),
        scratch_shapes=[pltpu.VMEM(s, F32) if isinstance(s, tuple) else s for s in scratch],
        compiler_params=pltpu.CompilerParams(vmem_limit_bytes=16 * 1024 * 1024),
    )(*args)


def swapped(pieces, group, order=(3, 2, 1)):
    count = lax.axis_size("seq")
    got = list(pieces)
    for i in order:
        got[i] = lax.ppermute(pieces[i], "seq", [(d, d ^ i) for d in range(count)])
    return got


def local(queries, keys, values, betas, gain, out_grad):
    tokens, heads, dim = queries.shape
    substeps = keys.shape[1]
    steps = tokens * substeps
    group = GROUP
    count = lax.axis_size("seq")
    groups = count // group
    bind = functools.partial
    q2 = queries.reshape(tokens * heads, dim)
    g2 = out_grad.reshape(tokens * heads, dim)
    k2 = keys.reshape(steps * heads, dim)
    v2 = values.reshape(steps * heads, dim)
    packed = betas.transpose(1, 2, 0).reshape(substeps * heads, tokens)
    gain2 = gain.reshape(1, dim)
    in_hbm = pl.BlockSpec(memory_space=pltpu.HBM)

    *maps, ku, inverse, w, e, rates = call(
        bind(first_kernel, group),
        [f32(dim, 2 * dim)] * heads
        + [
            f32(heads, steps, dim),
            f32(heads, steps, steps),
            f32(heads, steps, dim),
            f32(heads, steps, dim),
            f32(steps, heads),
        ],
        pltpu.with_memory_space_constraint(k2, pltpu.HBM),
        pltpu.with_memory_space_constraint(v2, pltpu.HBM),
        packed,
        specs=[in_hbm, in_hbm, pl.BlockSpec(memory_space=pltpu.VMEM)],
        scratch=[pltpu.VMEM((steps * heads, dim), BF16)] * 2
        + [(steps * heads, dim)] * 2
        + [(heads, steps), pltpu.SemaphoreType.DMA((2,))],
    )
    got = swapped(maps, group, (1, 2, 3))
    qu, scores, qc, o_part, kx = call(
        bind(second_kernel, group),
        [
            f32(heads, tokens, dim),
            f32(heads, tokens, steps),
            f32(heads, tokens, dim),
            f32(heads, tokens, dim),
            f32(heads, steps, dim),
        ],
        q2,
        rates,
        ku,
        inverse,
        w,
        e,
        scratch=[(tokens * heads, dim)],
    )
    starts, total, by_place = call(
        bind(join_kernel, group),
        [f32(group, dim, dim), f32(dim, dim), f32(group, dim, 2 * dim)],
        *got,
    )
    ahead = [(d, d + group) for d in range(count - group)]
    behind = [(d + group, d) for d in range(count - group)]
    across = [(d, d ^ group) for d in range(count)]
    two = groups == 2
    entry = lax.ppermute(total, "seq", across if two else ahead)
    before, after = call(
        bind(products_kernel, group), [f32(group + 1, dim, dim), f32(group, dim, dim)], by_place
    )
    for _ in range(groups - 2):
        passed = jnp.dot(before[group], entry, precision=lax.Precision.HIGHEST) + total
        entry = lax.ppermute(passed, "seq", ahead)
    states = call(
        bind(spread_kernel, group, 1 if two else None, False),
        [f32(dim, dim)] * heads,
        entry,
        starts,
        before,
    )
    states = swapped(states, group)
    *parts, normed, o_grad, err, gain_part = call(
        bind(read_kernel, group),
        [f32(dim, dim)] * heads
        + [
            out(BF16, tokens * heads, dim),
            f32(heads, tokens, dim),
            f32(heads, steps, dim),
            f32(8, dim),
        ],
        *states,
        g2,
        gain2,
        qc,
        o_part,
        w,
        e,
        scratch=[(tokens * heads, dim)] * 2,
    )
    got_parts = swapped(parts, group)
    head_count = lax.axis_size("head")
    hops = 1
    while two and hops < head_count:
        gain_part = gain_part + lax.ppermute(
            gain_part, "head", [(d, d ^ hops) for d in range(head_count)]
        )
        hops *= 2
    dq, dk0, z0 = call(
        bind(early_kernel, group),
        [out(BF16, tokens * heads, dim), f32(heads, steps, dim), f32(heads, steps, dim)],
        *states,
        q2,
        rates,
        o_grad,
        err,
        qu,
        ku,
        scores,
        inverse,
        scratch=[(tokens * heads, dim)] * 2,
    )
    starts, total = call(
        bind(join_back_kernel, group),
        [f32(group, dim, dim), f32(dim + 8, dim)],
        *got_parts,
        by_place,
        gain_part,
        scratch=[(group, dim, dim)],
    )
    entry = lax.ppermute(total, "seq", across if two else behind)
    for _ in range(groups - 2):
        passed = (
            jnp.dot(before[group].T, entry[:dim], precision=lax.Precision.HIGHEST) + total[:dim]
        )
        entry = lax.ppermute(jnp.pad(passed, ((0, 8), (0, 0))), "seq", behind)
    adjoints = call(
        bind(spread_back_kernel, group, 0 if two else None),
        [f32(dim + 8, dim)] * heads,
        entry,
        starts,
        after,
        gain_part,
    )
    adjoints = swapped(adjoints, group)
    dk, dv, db, gain_sum = call(
        bind(last_kernel, group),
        [
            out(BF16, steps * heads, dim),
            out(BF16, steps * heads, dim),
            out(F32, substeps * heads, tokens),
            out(F32, 8, dim),
        ],
        *adjoints,
        *states,
        k2,
        rates,
        ku,
        kx,
        err,
        z0,
        dk0,
        scratch=[(steps * heads, dim)] * 3,
    )
    gain_sum = gain_sum[0] if two else lax.psum(gain_part[0], ("seq", "head"))
    return (
        normed.reshape(tokens, heads, dim),
        dq.reshape(tokens, heads, dim),
        dk.reshape(tokens, substeps, heads, dim),
        dv.reshape(tokens, substeps, heads, dim),
        db.reshape(substeps, heads, tokens).transpose(2, 0, 1),
        gain_sum,
    )


def solution(mesh):
    return jax.shard_map(
        local,
        mesh=mesh,
        in_specs=(
            P("seq", "head", None),
            P("seq", None, "head", None),
            P("seq", None, "head", None),
            P("seq", None, "head"),
            P(),
            P("seq", "head", None),
        ),
        out_specs=(
            P("seq", "head", None),
            P("seq", "head", None),
            P("seq", None, "head", None),
            P("seq", None, "head", None),
            P("seq", None, "head"),
            P(),
        ),
        check_vma=False,
    )
```

```python
import functools
import types

import jax
import jax.numpy as jnp
from jax import lax
from jax.experimental import pallas as pl
from jax.experimental.pallas import tpu as pltpu
from jax.sharding import PartitionSpec as P

EPS = 1e-06
GROUP = 4
HALF = 128
BASE = 16
F32 = jnp.float32
BF16 = jnp.bfloat16


def split(x):
    high = x.astype(BF16)
    return high, (x - high.astype(F32)).astype(BF16)


def mm(a, b, ta=False, tb=False):
    (ah, al), (bh, bl) = split(a), split(b)
    if ta:
        ah, al = ah.T, al.T
    dims = (((1,), (1 if tb else 0,)), ((), ()))
    if b.shape[0 if tb else 1] > 128:
        left = jnp.concatenate([ah, ah, al], axis=1)
        right = jnp.concatenate([bh, bl, bh], axis=1 if tb else 0)
        return lax.dot_general(left, right, dims, preferred_element_type=F32)
    left = jnp.concatenate([ah, al], axis=1)
    if tb:
        right = jnp.concatenate(
            [jnp.concatenate([bh, bh], axis=1), jnp.concatenate([bl, bl], axis=1)], axis=0
        )
        width = b.shape[0]
    else:
        right = jnp.concatenate([bh, bl], axis=1)
        right = jnp.concatenate([right, right], axis=0)
        width = b.shape[1]
    both = lax.dot_general(left, right, dims, preferred_element_type=F32)
    return both[:, :width] + both[:, width:]


def exact_nt(a, b):
    return lax.dot_general(a, b, (((1,), (1,)), ((), ())), preferred_element_type=F32)


def iota(shape, dim):
    return lax.broadcasted_iota(jnp.int32, shape, dim)


def row_of(column):
    square = jnp.where(iota((HALF, HALF), 0) == iota((HALF, HALF), 1), column, 0.0)
    return jnp.sum(square, axis=0, keepdims=True)


def places(steps, j):
    shape = (steps, steps // 2)
    return (iota(shape, 0) == 2 * iota(shape, 1) + j).astype(F32)


def pick(a, b, ta=False, tb=False):
    dims = (((0 if ta else 1,), (1 if tb else 0,)), ((), ()))
    return lax.dot_general(
        a, b, dims, precision=lax.Precision.HIGHEST, preferred_element_type=F32
    )


def rate_column(rates, head):
    return jnp.sum(jnp.where(iota(rates.shape, 1) == head, rates, 0.0), axis=1, keepdims=True)


def small_inverses(lowers, rate_rows):
    blocks = HALF // BASE
    lane = iota((BASE, HALF), 1)
    row = iota((BASE, HALF), 0)
    jobs = range(len(lowers))
    packed = []
    for lower in lowers:
        one = lower[:BASE]
        for b in range(1, blocks):
            one = jnp.where(lane // BASE == b, lower[b * BASE : (b + 1) * BASE], one)
        packed.append(one)
    scaled = [packed[n] * rate_rows[n] for n in jobs]
    for j in range(BASE - 1):
        index = lane // BASE * BASE + j
        factors = [
            jnp.take_along_axis(scaled[n], index, axis=1, mode="promise_in_bounds") for n in jobs
        ]
        packed = [
            packed[n] - jnp.where(row > j, factors[n], 0.0) * packed[n][j : j + 1] for n in jobs
        ]
    return [
        jnp.concatenate(
            [jnp.where(lane // BASE == b, one, 0.0) for b in range(blocks)], axis=0
        )
        for one in packed
    ]


def place_in(group):
    return lax.rem(lax.axis_index("seq"), group)


def strided(ref, head, rows):
    return ref[pl.ds(head, rows, stride=ref.shape[0] // rows), :]


def store_strided(ref, head, value):
    rows = value.shape[0]
    ref[pl.ds(head, rows, stride=ref.shape[0] // rows), :] = value


SOONER, LATER = (1, 2), (3, 0)


def take(pairs, heads):
    order = SOONER + LATER
    return [pairs[order.index(h) // 2][order.index(h) % 2] for h in heads]


def inverse_norm(rows):
    return lax.rsqrt(jnp.sum(rows * rows, axis=1, keepdims=True) + EPS)


def unit_grad(inv, unit, grad):
    return inv * (grad - unit * jnp.sum(unit * grad, axis=1, keepdims=True))


def chunk(me, heads, kf, vf, rates, rows, o, wait):
    steps = rates.shape[0]
    strict = iota((HALF, HALF), 1) < iota((HALF, HALF), 0)
    rate = [rate_column(rates, me ^ h) for h in heads]
    rate_rows = [rows[pl.ds(me ^ h, 1), :] for h in heads]
    sides = [slice(0, HALF), slice(HALF, 2 * HALF)]
    raws = [strided(kf, me ^ h, steps) for h in heads]
    heads = range(len(heads)) if wait is None else heads
    count = range(len(raws))
    invs = [inverse_norm(raw) for raw in raws]
    inv_rows = [[row_of(inv[side]) for side in sides] for inv in invs]
    units = [raw * inv for raw, inv in zip(raws, invs)]
    raw16 = [raw.astype(BF16) for raw in raws]
    jobs = [(i, b) for i in count for b in range(2)]
    diag = {
        (i, b): jnp.where(
            strict,
            exact_nt(raw16[i][sides[b]], raw16[i][sides[b]]) * invs[i][sides[b]] * inv_rows[i][b],
            0.0,
        )
        for i, b in jobs
    }
    cross = [
        exact_nt(raw16[i][sides[1]], raw16[i][sides[0]]) * invs[i][sides[1]] * inv_rows[i][0]
        for i in count
    ]
    across = {(i, b): rate_rows[i][:, sides[b]] for i, b in jobs}
    inverse = dict(zip(jobs, small_inverses([diag[n] for n in jobs], [across[n] for n in jobs])))
    size = BASE
    while size < HALF:
        r, c = iota((HALF, HALF), 0) // size, iota((HALF, HALF), 1) // size
        below = (r % 2 == 1) & (c == r - 1)
        part = {n: jnp.where(below, diag[n], 0.0) for n in jobs}
        right = {n: part[n] - mm(part[n] * across[n], inverse[n]) for n in jobs}
        inverse = {
            n: inverse[n] + right[n] - mm(inverse[n] * across[n], right[n]) for n in jobs
        }
        size *= 2
    right = [cross[i] - mm(cross[i] * across[i, 0], inverse[i, 0]) for i in count]
    joined = [right[i] - mm(inverse[i, 1] * across[i, 1], right[i]) for i in count]
    vals = vf()
    both = [jnp.concatenate([units[i], vals[i]], axis=1) for i in count]
    top = [both[i][:HALF] - mm(inverse[i, 0] * across[i, 0], both[i][:HALF]) for i in count]
    low = [
        jnp.concatenate([joined[i] * across[i, 0], inverse[i, 1] * across[i, 1]], axis=1)
        for i in count
    ]
    bottom = [both[i][HALF:] - mm(low[i], both[i]) for i in count]
    solved = [jnp.concatenate([top[i], bottom[i]], axis=0) for i in count]
    eye = (iota((HALF, 2 * HALF), 0) == iota((HALF, 2 * HALF), 1)).astype(F32)
    sign = jnp.where(iota((HALF, 2 * HALF), 1) < HALF, -1.0, 1.0)
    ends = [eye + sign * mm(units[i], rate[i] * solved[i], ta=True) for i in count]
    for i in count:
        o.maps[i][...] = ends[i]
        o.unit[i] = units[i]
        o.inverse[i, :HALF, :HALF] = inverse[i, 0]
        o.inverse[i, :HALF, HALF:] = jnp.zeros((HALF, HALF), F32)
        o.inverse[i, HALF:, :HALF] = joined[i]
        o.inverse[i, HALF:, HALF:] = inverse[i, 1]
        o.w[i] = solved[i][:, :HALF]
        o.e[i] = solved[i][:, HALF:]


def first_kernel(group, heads, n, o, k16, v16, p32, sems):
    copies = [
        pltpu.make_async_copy(src, dst, sems.at[c])
        for c, (src, dst) in enumerate(((n.packed, p32), (n.k, k16), (n.v, v16)))
    ]
    for copy in copies:
        copy.start()
    me = place_in(group)
    steps, count = o.rates.shape
    copies[0].wait()
    packed = p32[...]
    own, place = [packed[:count], packed[count:]], [places(steps, j) for j in range(2)]
    rates = pick(place[0], own[0], tb=True) + pick(place[1], own[1], tb=True)
    o.rates[...] = rates
    o.rows[...] = pick(own[0], place[0], tb=True) + pick(own[1], place[1], tb=True)
    copies[1].wait()
    o.kf[...] = k16[...].astype(F32)
    copies[2].wait()
    o.vf[...] = v16[...].astype(F32)
    vals = [strided(o.vf, me ^ h, steps) for h in heads]
    chunk(me, heads, o.kf, lambda: vals, rates, o.rows, o, None)


def next_kernel(group, heads, n, o):
    me = place_in(group)
    steps = n.rates.shape[0]
    vals = [strided(n.vf, me ^ h, steps) for h in heads]
    chunk(me, heads, n.kf, lambda: vals, n.rates[...], n.rows, o, None)


def second_kernel(group, n, o, qf):
    me = place_in(group)
    qf[...] = n.q[...].astype(F32)
    heads, tokens, steps = o.scores.shape
    heads = range(heads)
    rates = n.rates[...]
    seen = iota((tokens, steps), 1) <= 2 * iota((tokens, steps), 0) + 1
    raws = [strided(qf, me ^ i, tokens) for i in heads]
    keys, w, e, inverse = (take(x, heads) for x in (n.unit, n.w, n.e, n.inverse))
    rate = [rate_column(rates, me ^ i) for i in heads]
    weighted = [rate[i] * jnp.concatenate([w[i], e[i]], axis=1) for i in heads]
    units = [raw * inverse_norm(raw) for raw in raws]
    scores = [jnp.where(seen, mm(units[i], keys[i], tb=True), 0.0) for i in heads]
    rows = [mm(scores[i], weighted[i]) for i in heads]
    spread = [keys[i] - mm(inverse[i], rate[i] * keys[i], ta=True) for i in heads]
    for i in heads:
        o.q_unit[i] = units[i]
        o.scores[i] = scores[i]
        o.qc[i] = units[i] - rows[i][:, :HALF]
        o.part[i] = rows[i][:, HALF:]
        o.kx[i] = spread[i]
    o.gain[...] = n.gain[...]


def join_kernel(group, n, o):
    me = place_in(group)
    for i, piece in enumerate(n.maps):
        o.maps[me ^ i] = piece[...]
    state = jnp.zeros((HALF, HALF), F32)
    for j in range(group):
        o.starts[j] = state
        own = o.maps[j, :, HALF:]
        state = own if j == 0 else mm(o.maps[j, :, :HALF], state) + own
    o.total[...] = state


def products_kernel(group, n, o):
    eye = (iota((HALF, HALF), 0) == iota((HALF, HALF), 1)).astype(F32)
    steps = [n.maps[j, :, :HALF] for j in range(group)]
    before, after = [eye, steps[0]], [eye, steps[-1]]
    for j in range(1, group):
        before.append(mm(steps[j], before[-1]))
        after.append(mm(after[-1], steps[-1 - j]))
    for j in range(group + 1):
        o.before[j] = before[j]
    for j in range(group):
        o.after[j] = after[group - 1 - j]


def spread_kernel(group, side, transposed, n, o):
    me = place_in(group)
    entry = n.entry[:HALF, :]
    if side is not None:
        entry = jnp.where(lax.axis_index("seq") // group == side, entry, 0.0)
    starts = [n.starts[me ^ i] for i in range(group)]
    maps = [n.maps[me ^ i] for i in range(group)]
    values = [starts[i] + mm(maps[i], entry, ta=transposed) for i in range(group)]
    for i, out in enumerate(o.states):
        out[:HALF, :] = values[i]
        if transposed:
            out[HALF:, :] = n.gain[...] + n.entry[HALF:, :]


def read_kernel(group, heads, n, o, gf, *of):
    me = place_in(group)
    gf[...] = n.og[...].astype(F32)
    tokens = n.qc.shape[1]
    gain = n.gain[...]
    given = [strided(gf, me ^ h, tokens) for h in heads]
    query = [n.qc[h] for h in heads]
    count = range(len(heads))
    reads = [n.part[h] + mm(query[i], n.states[i][...]) for i, h in enumerate(heads)]
    inv_rms = [lax.rsqrt(jnp.mean(read * read, axis=1, keepdims=True) + EPS) for read in reads]
    normal = [reads[i] * inv_rms[i] for i in count]
    scaled = [given[i] * gain for i in count]
    grads = [
        inv_rms[i] * (scaled[i] - normal[i] * jnp.mean(scaled[i] * normal[i], axis=1, keepdims=True))
        for i in count
    ]
    parts = [mm(query[i], grads[i], ta=True) for i in count]
    gain_part = sum(jnp.sum(given[i] * normal[i], axis=0, keepdims=True) for i in count)
    for i in count:
        o.parts[i][...] = parts[i]
        o.grad[i] = grads[i]
    if of:
        for i, h in enumerate(heads):
            store_strided(of[0], me ^ h, gain * normal[i])
            store_strided(of[0], me ^ SOONER[i], n.normed[i])
        o.normed[...] = of[0][...].astype(BF16)
        o.gain_part[...] = n.gain_part[...] + gain_part
    else:
        for i in count:
            o.normed[i] = gain * normal[i]
        o.gain_part[...] = jnp.broadcast_to(gain_part, o.gain_part.shape)


def query_kernel(group, n, o, qf, df):
    me = place_in(group)
    qf[...] = n.q[...].astype(F32)
    heads, tokens, steps = o.d_scores.shape
    heads = range(heads)
    rates = n.rates[...]
    seen = iota((tokens, steps), 1) <= 2 * iota((tokens, steps), 0) + 1
    raws = [strided(qf, me ^ i, tokens) for i in heads]
    states = [ref[...] for ref in n.states]
    grads, keys, w, e = (take(x, heads) for x in (n.grad, n.unit, n.w, n.e))
    units = [n.q_unit[i] for i in heads]
    errs = [e[i] - mm(w[i], states[i]) for i in heads]
    pseudo = [rate_column(rates, me ^ i) * errs[i] for i in heads]
    d_scores = [jnp.where(seen, mm(grads[i], pseudo[i], tb=True), 0.0) for i in heads]
    d_units = [mm(grads[i], states[i], tb=True) + mm(d_scores[i], keys[i]) for i in heads]
    done = [unit_grad(inverse_norm(raws[i]), units[i], d_units[i]) for i in heads]
    for i in heads:
        o.err[i] = errs[i]
        o.d_scores[i] = d_scores[i]
        store_strided(df, me ^ i, done[i])
    o.dq[...] = df[...].astype(BF16)


def early_kernel(group, n, o):
    me = place_in(group)
    heads = range(o.dk.shape[0])
    rates = n.rates[...]
    rate = [rate_column(rates, me ^ i) for i in heads]
    grads, inverse = (take(x, heads) for x in (n.grad, n.inverse))
    units, scores, d_scores = ([x[i] for i in heads] for x in (n.q_unit, n.scores, n.d_scores))
    d_keys = [mm(d_scores[i], units[i], ta=True) for i in heads]
    d_pseudo = [mm(scores[i], grads[i], ta=True) for i in heads]
    z = [d_pseudo[i] - mm(inverse[i], rate[i] * d_pseudo[i], ta=True) for i in heads]
    for i in heads:
        o.dk[i] = d_keys[i]
        o.z[i] = z[i]


def join_back_kernel(group, n, o, parts):
    me = place_in(group)
    for i, piece in enumerate(n.parts):
        parts[me ^ i] = piece[...]
    maps = [n.maps[j, :, :HALF] for j in range(group)]
    adjoint = jnp.zeros((HALF, HALF), F32)
    for j in reversed(range(group)):
        o.starts[j] = adjoint
        own = parts[j]
        adjoint = own if j == group - 1 else mm(maps[j], adjoint, ta=True) + own
    o.total[:HALF, :] = adjoint
    gain = sum(ref[...] for ref in n.gains)
    o.total[HALF:, :] = gain
    o.gain[...] = gain


def last_kernel(group, heads, n, o, kf, *scratch):
    me = place_in(group)
    kf[...] = n.k[...].astype(F32)
    rates = n.rates[...]
    steps, every = rates.shape
    count = range(len(heads))
    rate = [rate_column(rates, me ^ h) for h in heads]
    raws = [strided(kf, me ^ h, steps) for h in heads]
    adjoints = [ref[:HALF, :] for ref in n.adjoints]
    states = [ref[...] for ref in n.states]
    units = take(n.unit, heads)
    errs, kx, z0, dk0 = ([x[h] for h in heads] for x in (n.err, n.kx, n.z, n.dk))
    z = [z0[i] + mm(kx[i], adjoints[i]) for i in count]
    invs = [inverse_norm(raw) for raw in raws]
    pseudo = [rate[i] * errs[i] for i in count]
    d_values = [rate[i] * z[i] for i in count]
    below = iota((steps, steps), 1) < iota((steps, steps), 0)
    above = iota((steps, steps), 1) > iota((steps, steps), 0)
    d_grams = [
        jnp.where(
            below,
            mm(d_values[i], pseudo[i], tb=True),
            jnp.where(above, mm(pseudo[i], d_values[i], tb=True), 0.0),
        )
        for i in count
    ]
    d_units = [
        dk0[i]
        + mm(pseudo[i], adjoints[i], tb=True)
        - mm(d_values[i], states[i], tb=True)
        - mm(d_grams[i], units[i])
        for i in count
    ]
    done = [unit_grad(invs[i], units[i], d_units[i]) for i in count]
    d_rates = n.d_rates[...] if scratch else jnp.zeros(rates.shape, F32)
    for i, h in enumerate(heads):
        d_rate = jnp.sum(z[i] * errs[i], axis=1, keepdims=True)
        d_rates = jnp.where(iota(rates.shape, 1) == me ^ h, d_rate, d_rates)
    if not scratch:
        for i in count:
            o.dk[i] = done[i]
            o.dv[i] = d_values[i]
        o.d_rates[...] = d_rates
        return
    df, vf = scratch
    for i, h in enumerate(heads):
        store_strided(vf, me ^ SOONER[i], n.dv[i])
        store_strided(vf, me ^ h, d_values[i])
        store_strided(df, me ^ SOONER[i], n.dk1[i])
        store_strided(df, me ^ h, done[i])
    o.dk[...] = df[...].astype(BF16)
    o.dv[...] = vf[...].astype(BF16)
    for j in range(2):
        o.db[j * every : (j + 1) * every, :] = pick(d_rates, places(steps, j), ta=True)
    o.gain[...] = sum(ref[HALF:, :] for ref in n.all_adjoints)[:1]


def f32(*shape):
    return pltpu.VMEM(shape, F32)


def out(dtype, *shape):
    return jax.ShapeDtypeStruct(shape, dtype)


def call(body, ins, outs, scratch=(), hbm=(), after=(), flops=1000):
    names = [name for name in ins]
    flat, tree = jax.tree.flatten([ins[name] for name in names])
    outs = dict(outs)
    flat_outs, out_tree = jax.tree.flatten(outs)
    specs = jax.tree.leaves(
        [
            jax.tree.map(
                lambda _: pl.BlockSpec(memory_space=pltpu.HBM if name in hbm else pltpu.VMEM),
                ins[name],
            )
            for name in names
        ]
    )
    after = list(after)

    def kernel(*refs):
        values = jax.tree.unflatten(tree, refs[: len(flat)])
        start = len(flat) + len(after)
        results = jax.tree.unflatten(out_tree, refs[start : start + len(flat_outs)])
        body(
            types.SimpleNamespace(**dict(zip(names, values))),
            types.SimpleNamespace(**results),
            *refs[start + len(flat_outs) :],
        )

    results = pl.pallas_call(
        kernel,
        out_shape=flat_outs,
        in_specs=specs + [pl.BlockSpec(memory_space=pl.ANY)] * len(after),
        scratch_shapes=[pltpu.VMEM(s, F32) if isinstance(s, tuple) else s for s in scratch],
        compiler_params=pltpu.CompilerParams(vmem_limit_bytes=16 * 1024 * 1024),
        cost_estimate=pl.CostEstimate(flops=flops, bytes_accessed=0, transcendentals=0),
    )(*flat, *after)
    return types.SimpleNamespace(**jax.tree.unflatten(out_tree, results))


def swap(piece, i):
    return lax.ppermute(piece, "seq", [(d, d ^ i) for d in range(lax.axis_size("seq"))])


def local(queries, keys, values, betas, gain, out_grad):
    tokens, heads, dim = queries.shape
    substeps = keys.shape[1]
    steps = tokens * substeps
    group = GROUP
    count = lax.axis_size("seq")
    groups = count // group
    two = groups == 2
    bind = functools.partial
    q2 = queries.reshape(tokens * heads, dim)
    g2 = out_grad.reshape(tokens * heads, dim)
    k2 = keys.reshape(steps * heads, dim)
    v2 = values.reshape(steps * heads, dim)
    packed = betas.transpose(1, 2, 0).reshape(substeps * heads, tokens)

    def chunk_outs():
        return dict(
            maps=[f32(dim, 2 * dim) for _ in SOONER],
            unit=f32(2, steps, dim),
            inverse=f32(2, steps, steps),
            w=f32(2, steps, dim),
            e=f32(2, steps, dim),
        )

    a = call(
        bind(first_kernel, group, SOONER),
        {
            name: pltpu.with_memory_space_constraint(x, pltpu.HBM)
            for name, x in (("k", k2), ("v", v2), ("packed", packed))
        },
        dict(
            chunk_outs(),
            rates=f32(steps, heads),
            rows=f32(heads, steps),
            kf=f32(steps * heads, dim),
            vf=f32(steps * heads, dim),
        ),
        scratch=[pltpu.VMEM((steps * heads, dim), BF16)] * 2
        + [(substeps * heads, tokens), pltpu.SemaphoreType.DMA((3,))],
        hbm=("k", "v", "packed"),
    )
    got = {h: swap(a.maps[i], h) for i, h in enumerate(SOONER)}
    b = call(
        bind(next_kernel, group, LATER),
        dict(kf=a.kf, vf=a.vf, rates=a.rates, rows=a.rows),
        chunk_outs(),
    )
    for i, h in enumerate(LATER):
        got[h] = swap(b.maps[i], h) if h else b.maps[i]
    unit, inverse, w, e = ([getattr(x, name) for x in (a, b)] for name in ("unit", "inverse", "w", "e"))
    rates = a.rates
    c = call(
        bind(second_kernel, group),
        dict(q=q2, gain=gain.reshape(1, dim), rates=rates, unit=unit, inverse=inverse, w=w, e=e),
        dict(
            q_unit=f32(heads, tokens, dim),
            scores=f32(heads, tokens, steps),
            qc=f32(heads, tokens, dim),
            part=f32(heads, tokens, dim),
            kx=f32(heads, steps, dim),
            gain=f32(1, dim),
        ),
        scratch=[(tokens * heads, dim)],
        after=[got[h] for h in SOONER],
        flops=10**9,
    )
    j = call(
        bind(join_kernel, group),
        dict(maps=[got[h] for h in range(heads)]),
        dict(
            starts=f32(group, dim, dim), total=f32(dim, dim), maps=f32(group, dim, 2 * dim)
        ),
        after=[c.gain],
    )
    ahead = [(d, d + group) for d in range(count - group)]
    behind = [(d + group, d) for d in range(count - group)]
    across = [(d, d ^ group) for d in range(count)]
    entry = lax.ppermute(j.total, "seq", across if two else ahead)
    p = call(
        bind(products_kernel, group),
        dict(maps=j.maps),
        dict(before=f32(group + 1, dim, dim), after=f32(group, dim, dim)),
    )
    for _ in range(groups - 2):
        passed = jnp.dot(p.before[group], entry, precision=lax.Precision.HIGHEST) + j.total
        entry = lax.ppermute(passed, "seq", ahead)
    states = call(
        bind(spread_kernel, group, 1 if two else None, False),
        dict(entry=entry, starts=j.starts, maps=p.before),
        dict(states=[f32(dim, dim)] * heads),
    ).states
    states = [states[0]] + [swap(states[h], h) for h in range(1, heads)]
    shared = dict(og=g2, gain=c.gain, qc=c.qc, part=c.part)
    r1 = call(
        bind(read_kernel, group, SOONER),
        dict(shared, states=[states[h] for h in SOONER]),
        dict(
            parts=[f32(dim, dim)] * 2,
            grad=f32(2, tokens, dim),
            normed=f32(2, tokens, dim),
            gain_part=f32(8, dim),
        ),
        scratch=[(tokens * heads, dim)],
    )
    got = {h: swap(r1.parts[i], h) for i, h in enumerate(SOONER)}
    r2 = call(
        bind(read_kernel, group, LATER),
        dict(
            shared,
            states=[states[h] for h in LATER],
            normed=r1.normed,
            gain_part=r1.gain_part,
        ),
        dict(
            parts=[f32(dim, dim)] * 2,
            grad=f32(2, tokens, dim),
            normed=out(BF16, tokens * heads, dim),
            gain_part=f32(8, dim),
        ),
        scratch=[(tokens * heads, dim)] * 2,
    )
    for i, h in enumerate(LATER):
        got[h] = swap(r2.parts[i], h) if h else r2.parts[i]
    grad = [r1.grad, r2.grad]
    gain_part = r2.gain_part
    gains = [gain_part]
    if two:
        size = lax.axis_size("head")
        if size > 1:
            gain_part = gain_part + lax.ppermute(
                gain_part, "head", [(d, d ^ 1) for d in range(size)]
            )
        gains = [gain_part] + [
            lax.ppermute(gain_part, "head", [(d, d ^ flip) for d in range(size)])
            for flip in range(2, size, 2)
        ]
    y = call(
        bind(query_kernel, group),
        dict(
            states=states,
            q=q2,
            rates=rates,
            grad=grad,
            w=w,
            e=e,
            q_unit=c.q_unit,
            unit=unit,
        ),
        dict(
            dq=out(BF16, tokens * heads, dim),
            err=f32(heads, steps, dim),
            d_scores=f32(heads, tokens, steps),
        ),
        scratch=[(tokens * heads, dim)] * 2,
        after=[got[h] for h in SOONER],
        flops=10**9,
    )
    jb = call(
        bind(join_back_kernel, group),
        dict(parts=[got[h] for h in range(heads)], maps=j.maps, gains=gains),
        dict(starts=f32(group, dim, dim), total=f32(dim + 8, dim), gain=f32(8, dim)),
        scratch=[(group, dim, dim)],
        after=[y.err],
    )
    entry = lax.ppermute(jb.total, "seq", across if two else behind)
    z = call(
        bind(early_kernel, group),
        dict(
            rates=rates,
            grad=grad,
            d_scores=y.d_scores,
            q_unit=c.q_unit,
            scores=c.scores,
            inverse=inverse,
        ),
        dict(dk=f32(heads, steps, dim), z=f32(heads, steps, dim)),
    )
    for _ in range(groups - 2):
        passed = jnp.dot(p.before[group].T, entry[:dim], precision=lax.Precision.HIGHEST)
        entry = lax.ppermute(jb.total.at[:dim].add(passed), "seq", behind)
    adjoints = call(
        bind(spread_kernel, group, 0 if two else None, True),
        dict(entry=entry, starts=jb.starts, maps=p.after, gain=jb.gain),
        dict(states=[f32(dim + 8, dim)] * heads),
        after=[z.dk],
    ).states
    adjoints = [adjoints[0]] + [swap(adjoints[h], h) for h in range(1, heads)]
    ins = dict(
        k=k2, rates=rates, unit=unit, err=y.err, kx=c.kx, z=z.z, dk=z.dk
    )
    l1 = call(
        bind(last_kernel, group, SOONER),
        dict(ins, adjoints=[adjoints[h] for h in SOONER], states=[states[h] for h in SOONER]),
        dict(dk=f32(2, steps, dim), dv=f32(2, steps, dim), d_rates=f32(steps, heads)),
        scratch=[(steps * heads, dim)],
    )
    l2 = call(
        bind(last_kernel, group, LATER),
        dict(
            ins,
            adjoints=[adjoints[h] for h in LATER],
            states=[states[h] for h in LATER],
            all_adjoints=adjoints,
            dk1=l1.dk,
            dv=l1.dv,
            d_rates=l1.d_rates,
        ),
        dict(
            dk=out(BF16, steps * heads, dim),
            dv=out(BF16, steps * heads, dim),
            db=out(F32, substeps * heads, tokens),
            gain=out(F32, 1, dim),
        ),
        scratch=[(steps * heads, dim)] * 3,
    )
    gain_sum = l2.gain[0] if two else lax.psum(gain_part[0], ("seq", "head"))
    return (
        r2.normed.reshape(tokens, heads, dim),
        y.dq.reshape(tokens, heads, dim),
        l2.dk.reshape(tokens, substeps, heads, dim),
        l2.dv.reshape(tokens, substeps, heads, dim),
        l2.db.reshape(substeps, heads, tokens).transpose(2, 0, 1),
        gain_sum,
    )


def solution(mesh):
    return jax.shard_map(
        local,
        mesh=mesh,
        in_specs=(
            P("seq", "head", None),
            P("seq", None, "head", None),
            P("seq", None, "head", None),
            P("seq", None, "head"),
            P(),
            P("seq", "head", None),
        ),
        out_specs=(
            P("seq", "head", None),
            P("seq", "head", None),
            P("seq", None, "head", None),
            P("seq", None, "head", None),
            P("seq", None, "head"),
            P(),
        ),
        check_vma=False,
    )
```

```python
import functools
import types

import jax
import jax.numpy as jnp
from jax import lax
from jax.experimental import pallas as pl
from jax.experimental.pallas import tpu as pltpu
from jax.sharding import PartitionSpec as P

EPS = 1e-06
GROUP = 4
HALF = 128
BASE = 16
F32 = jnp.float32
BF16 = jnp.bfloat16


def split(x):
    high = x.astype(BF16)
    return high, (x - high.astype(F32)).astype(BF16)


def mm(a, b, ta=False, tb=False):
    (ah, al), (bh, bl) = split(a), split(b)
    if ta:
        ah, al = ah.T, al.T
    dims = (((1,), (1 if tb else 0,)), ((), ()))
    if b.shape[0 if tb else 1] > 128:
        left = jnp.concatenate([ah, ah, al], axis=1)
        right = jnp.concatenate([bh, bl, bh], axis=1 if tb else 0)
        return lax.dot_general(left, right, dims, preferred_element_type=F32)
    left = jnp.concatenate([ah, al], axis=1)
    if tb:
        right = jnp.concatenate(
            [jnp.concatenate([bh, bh], axis=1), jnp.concatenate([bl, bl], axis=1)], axis=0
        )
        width = b.shape[0]
    else:
        right = jnp.concatenate([bh, bl], axis=1)
        right = jnp.concatenate([right, right], axis=0)
        width = b.shape[1]
    both = lax.dot_general(left, right, dims, preferred_element_type=F32)
    return both[:, :width] + both[:, width:]


def exact_nt(a, b):
    return lax.dot_general(a, b, (((1,), (1,)), ((), ())), preferred_element_type=F32)


def iota(shape, dim):
    return lax.broadcasted_iota(jnp.int32, shape, dim)


def row_of(column):
    square = jnp.where(iota((HALF, HALF), 0) == iota((HALF, HALF), 1), column, 0.0)
    return jnp.sum(square, axis=0, keepdims=True)


def places(steps, j):
    shape = (steps, steps // 2)
    return (iota(shape, 0) == 2 * iota(shape, 1) + j).astype(F32)


def pick(a, b, ta=False, tb=False):
    dims = (((0 if ta else 1,), (1 if tb else 0,)), ((), ()))
    return lax.dot_general(
        a, b, dims, precision=lax.Precision.HIGHEST, preferred_element_type=F32
    )


def rate_column(rates, head):
    return jnp.sum(jnp.where(iota(rates.shape, 1) == head, rates, 0.0), axis=1, keepdims=True)


def small_inverses(lowers, rate_rows):
    blocks = HALF // BASE
    lane = iota((BASE, HALF), 1)
    row = iota((BASE, HALF), 0)
    jobs = range(len(lowers))
    packed = []
    for lower in lowers:
        one = lower[:BASE]
        for b in range(1, blocks):
            one = jnp.where(lane // BASE == b, lower[b * BASE : (b + 1) * BASE], one)
        packed.append(one)
    scaled = [packed[n] * rate_rows[n] for n in jobs]
    for j in range(BASE - 1):
        index = lane // BASE * BASE + j
        factors = [
            jnp.take_along_axis(scaled[n], index, axis=1, mode="promise_in_bounds") for n in jobs
        ]
        packed = [
            packed[n] - jnp.where(row > j, factors[n], 0.0) * packed[n][j : j + 1] for n in jobs
        ]
    return [
        jnp.concatenate(
            [jnp.where(lane // BASE == b, one, 0.0) for b in range(blocks)], axis=0
        )
        for one in packed
    ]


def place_in(group):
    return lax.rem(lax.axis_index("seq"), group)


def strided(ref, head, rows):
    return ref[pl.ds(head, rows, stride=ref.shape[0] // rows), :]


def store_strided(ref, head, value):
    rows = value.shape[0]
    ref[pl.ds(head, rows, stride=ref.shape[0] // rows), :] = value


SOONER, LATER = (1, 2), (3, 0)


def take(pairs, heads):
    order = SOONER + LATER
    return [pairs[order.index(h) // 2][order.index(h) % 2] for h in heads]


def inverse_norm(rows):
    return lax.rsqrt(jnp.sum(rows * rows, axis=1, keepdims=True) + EPS)


def unit_grad(inv, unit, grad):
    return inv * (grad - unit * jnp.sum(unit * grad, axis=1, keepdims=True))


def chunk(me, heads, kf, vf, rates, rows, o, wait):
    steps = rates.shape[0]
    strict = iota((HALF, HALF), 1) < iota((HALF, HALF), 0)
    rate = [rate_column(rates, me ^ h) for h in heads]
    rate_rows = [rows[pl.ds(me ^ h, 1), :] for h in heads]
    sides = [slice(0, HALF), slice(HALF, 2 * HALF)]
    raws = [strided(kf, me ^ h, steps) for h in heads]
    heads = range(len(heads)) if wait is None else heads
    count = range(len(raws))
    invs = [inverse_norm(raw) for raw in raws]
    inv_rows = [[row_of(inv[side]) for side in sides] for inv in invs]
    units = [raw * inv for raw, inv in zip(raws, invs)]
    raw16 = [raw.astype(BF16) for raw in raws]
    jobs = [(i, b) for i in count for b in range(2)]
    diag = {
        (i, b): jnp.where(
            strict,
            exact_nt(raw16[i][sides[b]], raw16[i][sides[b]]) * invs[i][sides[b]] * inv_rows[i][b],
            0.0,
        )
        for i, b in jobs
    }
    cross = [
        exact_nt(raw16[i][sides[1]], raw16[i][sides[0]]) * invs[i][sides[1]] * inv_rows[i][0]
        for i in count
    ]
    across = {(i, b): rate_rows[i][:, sides[b]] for i, b in jobs}
    inverse = dict(zip(jobs, small_inverses([diag[n] for n in jobs], [across[n] for n in jobs])))
    size = BASE
    while size < HALF:
        r, c = iota((HALF, HALF), 0) // size, iota((HALF, HALF), 1) // size
        below = (r % 2 == 1) & (c == r - 1)
        part = {n: jnp.where(below, diag[n], 0.0) for n in jobs}
        right = {n: part[n] - mm(part[n] * across[n], inverse[n]) for n in jobs}
        inverse = {
            n: inverse[n] + right[n] - mm(inverse[n] * across[n], right[n]) for n in jobs
        }
        size *= 2
    right = [cross[i] - mm(cross[i] * across[i, 0], inverse[i, 0]) for i in count]
    joined = [right[i] - mm(inverse[i, 1] * across[i, 1], right[i]) for i in count]
    vals = vf()
    both = [jnp.concatenate([units[i], vals[i]], axis=1) for i in count]
    top = [both[i][:HALF] - mm(inverse[i, 0] * across[i, 0], both[i][:HALF]) for i in count]
    low = [
        jnp.concatenate([joined[i] * across[i, 0], inverse[i, 1] * across[i, 1]], axis=1)
        for i in count
    ]
    bottom = [both[i][HALF:] - mm(low[i], both[i]) for i in count]
    solved = [jnp.concatenate([top[i], bottom[i]], axis=0) for i in count]
    eye = (iota((HALF, 2 * HALF), 0) == iota((HALF, 2 * HALF), 1)).astype(F32)
    sign = jnp.where(iota((HALF, 2 * HALF), 1) < HALF, -1.0, 1.0)
    ends = [eye + sign * mm(units[i], rate[i] * solved[i], ta=True) for i in count]
    for i in count:
        o.maps[i][:, : 2 * HALF] = ends[i]
        o.unit[i] = units[i]
        o.inverse[i, :HALF, :HALF] = inverse[i, 0]
        o.inverse[i, :HALF, HALF:] = jnp.zeros((HALF, HALF), F32)
        o.inverse[i, HALF:, :HALF] = joined[i]
        o.inverse[i, HALF:, HALF:] = inverse[i, 1]
        o.w[i] = solved[i][:, :HALF]
        o.e[i] = solved[i][:, HALF:]
    return units, [x[:, :HALF] for x in solved], [x[:, HALF:] for x in solved]


def first_kernel(group, heads, n, o, k16, v16, q16, g16, p32, sems):
    copies = [
        pltpu.make_async_copy(src, dst, sems.at[c])
        for c, (src, dst) in enumerate(
            (
                (n.packed, p32),
                (n.k, k16),
                (n.v, v16),
                (n.q, q16),
                (n.og, g16),
                (n.gain, o.gain),
            )
        )
    ]
    for copy in copies:
        copy.start()
    me = place_in(group)
    steps, count = o.rates.shape
    copies[0].wait()
    packed = p32[...]
    own, place = [packed[:count], packed[count:]], [places(steps, j) for j in range(2)]
    rates = pick(place[0], own[0], tb=True) + pick(place[1], own[1], tb=True)
    o.rates[...] = rates
    o.rows[...] = pick(own[0], place[0], tb=True) + pick(own[1], place[1], tb=True)
    copies[1].wait()
    o.kf[...] = k16[...].astype(F32)
    copies[2].wait()
    o.vf[...] = v16[...].astype(F32)
    for copy in copies[3:]:
        copy.wait()
    o.qf[...] = q16[...].astype(F32)
    o.gf[...] = g16[...].astype(F32)
    tokens = steps // 2
    vals = [strided(o.vf, me ^ h, steps) for h in heads]
    qs = [strided(o.qf, me ^ h, tokens) for h in heads]
    given = [strided(o.gf, me ^ h, tokens) for h in heads]
    solved = chunk(me, heads, o.kf, lambda: vals, rates, o.rows, o, None)
    reads(heads, qs, given, rates, *solved, me, o)


def next_kernel(group, heads, n, o):
    me = place_in(group)
    steps = n.rates.shape[0]
    vals = [strided(n.vf, me ^ h, steps) for h in heads]
    chunk(me, heads, n.kf, lambda: vals, n.rates[...], n.rows, o, None)


def reads(heads, qs, given, rates, keys, w, e, me, o):
    tokens = qs[0].shape[0]
    steps = 2 * tokens
    count = range(len(heads))
    seen = iota((tokens, steps), 1) <= 2 * iota((tokens, steps), 0) + 1
    rate = [rate_column(rates, me ^ h) for h in heads]
    weighted = [rate[i] * jnp.concatenate([w[i], e[i]], axis=1) for i in count]
    units = [q * inverse_norm(q) for q in qs]
    scores = [jnp.where(seen, mm(units[i], keys[i], tb=True), 0.0) for i in count]
    rows = [mm(scores[i], weighted[i]) for i in count]
    for i in count:
        o.q_unit[i] = units[i]
        o.scores[i] = scores[i]
        out = o.reads[i]
        skip = out.shape[1] - 3 * HALF
        out[:, skip : skip + HALF] = units[i] - rows[i][:, :HALF]
        out[:, skip + HALF : skip + 2 * HALF] = rows[i][:, HALF:]
        out[:, skip + 2 * HALF :] = given[i]


def second_kernel(group, heads, n, o):
    me = place_in(group)
    tokens = o.scores.shape[1]
    rates = n.rates[...]
    qs = [strided(n.qf, me ^ h, tokens) for h in heads]
    given = [strided(n.gf, me ^ h, tokens) for h in heads]
    keys, w, e = (take(x, heads) for x in (n.unit, n.w, n.e))
    every = range(o.kx.shape[0])
    rate = [rate_column(rates, me ^ i) for i in every]
    units, inverse = (take(x, every) for x in (n.unit, n.inverse))
    spread = [units[i] - mm(inverse[i], rate[i] * units[i], ta=True) for i in every]
    reads(heads, qs, given, rates, keys, w, e, me, o)
    for i in every:
        o.kx[i] = spread[i]


def join_kernel(group, n, o):
    me = place_in(group)
    for i, piece in enumerate(n.maps):
        o.maps[me ^ i] = piece[:, : 2 * HALF]
    state = jnp.zeros((HALF, HALF), F32)
    for j in range(group):
        o.starts[j] = state
        own = o.maps[j, :, HALF:]
        state = own if j == 0 else mm(o.maps[j, :, :HALF], state) + own
    o.total[...] = state


def products_kernel(group, n, o):
    eye = (iota((HALF, HALF), 0) == iota((HALF, HALF), 1)).astype(F32)
    steps = [n.maps[j, :, :HALF] for j in range(group)]
    before, after = [eye, steps[0]], [eye, steps[-1]]
    for j in range(1, group):
        before.append(mm(steps[j], before[-1]))
        after.append(mm(after[-1], steps[-1 - j]))
    for j in range(group + 1):
        o.before[j] = before[j]
    for j in range(group):
        o.after[j] = after[group - 1 - j]


def spread_kernel(group, side, n, o):
    me = place_in(group)
    entry = n.entry[:HALF, :]
    if side is not None:
        entry = jnp.where(lax.axis_index("seq") // group == side, entry, 0.0)
    starts = [n.starts[me ^ i] for i in range(group)]
    maps = [n.maps[me ^ i] for i in range(group)]
    values = [starts[i] + mm(maps[i], entry, ta=True) for i in range(group)]
    for i, out in enumerate(o.adjoints):
        out[:HALF, :] = values[i]
        out[HALF:, :] = n.entry[HALF:, :]


def normed_and_grads(queries, parts, states, given, gain):
    count = range(len(queries))
    reads = [parts[i] + mm(queries[i], states[i]) for i in count]
    inv_rms = [lax.rsqrt(jnp.mean(read * read, axis=1, keepdims=True) + EPS) for read in reads]
    normal = [reads[i] * inv_rms[i] for i in count]
    scaled = [given[i] * gain for i in count]
    grads = [
        inv_rms[i] * (scaled[i] - normal[i] * jnp.mean(scaled[i] * normal[i], axis=1, keepdims=True))
        for i in count
    ]
    return normal, grads, sum(jnp.sum(given[i] * normal[i], axis=0, keepdims=True) for i in count)


def owner_kernel(group, side, n, o, packed):
    me = place_in(group)
    entry = n.entry[...]
    if side is not None:
        entry = jnp.where(lax.axis_index("seq") // group == side, entry, 0.0)
    for i, piece in enumerate(n.reads):
        packed[me ^ i] = piece[:, piece.shape[1] - 3 * HALF :]
    gain = n.gain[...]
    places_ = range(group)
    maps = [n.maps[j, :, :HALF] for j in places_]
    before = [n.before[j] for j in places_]
    starts = [n.starts[j] for j in places_]
    queries, parts, given = (
        [packed[j, :, c * HALF : (c + 1) * HALF] for j in places_] for c in range(3)
    )
    states = [starts[j] + mm(before[j], entry) if j else starts[j] + entry for j in places_]
    _, grads, gain_part = normed_and_grads(queries, parts, states, given, gain)
    adjoints = [mm(queries[j], grads[j], ta=True) for j in places_]
    chain = [jnp.zeros((HALF, HALF), F32), adjoints[-1]]
    for j in reversed(range(group - 1)):
        chain.append(mm(maps[j], chain[-1], ta=True) + adjoints[j])
    for j in places_:
        o.starts[j] = chain[group - 1 - j]
        o.entries[j] = states[j]
    o.total[:HALF, :] = chain[-1]
    for i in places_:
        o.states[i][:HALF, :] = o.entries[me ^ i]
        o.states[i][HALF:, :] = jnp.broadcast_to(gain_part, (8, HALF))
    o.total[HALF:, :] = jnp.broadcast_to(gain_part, (8, HALF))


def tokens_kernel(group, n, o, of, df):
    me = place_in(group)
    heads, tokens, steps = range(len(n.reads)), n.reads[0].shape[0], n.rates.shape[0]
    gain = n.gain[...]
    rates = n.rates[...]
    queries, parts, given = (
        [
            ref[:, ref.shape[1] - (3 - c) * HALF : ref.shape[1] - (2 - c) * HALF]
            for ref in n.reads
        ]
        for c in range(3)
    )
    states = [ref[:HALF, :] for ref in n.states]
    seen = iota((tokens, steps), 1) <= 2 * iota((tokens, steps), 0) + 1
    raws = [strided(n.qf, me ^ i, tokens) for i in heads]
    keys, w, e, units, inverse, scores = (
        take(x, heads) for x in (n.unit, n.w, n.e, n.q_unit, n.inverse, n.scores)
    )
    rate = [rate_column(rates, me ^ i) for i in heads]
    invs = [inverse_norm(raw) for raw in raws]
    errs = [e[i] - mm(w[i], states[i]) for i in heads]
    normal, grads, _ = normed_and_grads(queries, parts, states, given, gain)
    pseudo = [rate[i] * errs[i] for i in heads]
    d_scores = [jnp.where(seen, mm(grads[i], pseudo[i], tb=True), 0.0) for i in heads]
    d_pseudo = [mm(scores[i], grads[i], ta=True) for i in heads]
    d_units = [mm(grads[i], states[i], tb=True) + mm(d_scores[i], keys[i]) for i in heads]
    z = [d_pseudo[i] - mm(inverse[i], rate[i] * d_pseudo[i], ta=True) for i in heads]
    d_keys = [mm(d_scores[i], units[i], ta=True) for i in heads]
    done = [unit_grad(invs[i], units[i], d_units[i]) for i in heads]
    for i in heads:
        o.err[i] = errs[i]
        o.dk[i] = d_keys[i]
        o.z[i] = z[i]
        store_strided(of, me ^ i, gain * normal[i])
        store_strided(df, me ^ i, done[i])
    o.normed[...] = of[...].astype(BF16)
    o.dq[...] = df[...].astype(BF16)


def gain_kernel(n, o):
    o.gain[...] = sum(ref[HALF : HALF + 1, :] for ref in n.states + n.adjoints)


def last_kernel(group, n, o, df, vf):
    me = place_in(group)
    rates = n.rates[...]
    steps, count = rates.shape
    heads = range(count)
    rate = [rate_column(rates, me ^ i) for i in heads]
    raws = [strided(n.kf, me ^ i, steps) for i in heads]
    adjoints = [ref[:HALF, :] for ref in n.adjoints]
    states = [ref[:HALF, :] for ref in n.states]
    units = take(n.unit, heads)
    errs, kx, z0, dk0 = ([x[i] for i in heads] for x in (n.err, n.kx, n.z, n.dk))
    z = [z0[i] + mm(kx[i], adjoints[i]) for i in heads]
    invs = [inverse_norm(raw) for raw in raws]
    pseudo = [rate[i] * errs[i] for i in heads]
    d_values = [rate[i] * z[i] for i in heads]
    below = iota((steps, steps), 1) < iota((steps, steps), 0)
    above = iota((steps, steps), 1) > iota((steps, steps), 0)
    d_grams = [
        jnp.where(
            below,
            mm(d_values[i], pseudo[i], tb=True),
            jnp.where(above, mm(pseudo[i], d_values[i], tb=True), 0.0),
        )
        for i in heads
    ]
    d_units = [
        dk0[i]
        + mm(pseudo[i], adjoints[i], tb=True)
        - mm(d_values[i], states[i], tb=True)
        - mm(d_grams[i], units[i])
        for i in heads
    ]
    done = [unit_grad(invs[i], units[i], d_units[i]) for i in heads]
    d_rates = jnp.zeros(rates.shape, F32)
    for i in heads:
        d_rate = jnp.sum(z[i] * errs[i], axis=1, keepdims=True)
        d_rates = jnp.where(iota(rates.shape, 1) == me ^ i, d_rate, d_rates)
        store_strided(vf, me ^ i, d_values[i])
        store_strided(df, me ^ i, done[i])
    o.dk[...] = df[...].astype(BF16)
    o.dv[...] = vf[...].astype(BF16)
    for j in range(2):
        o.db[j * count : (j + 1) * count, :] = pick(d_rates, places(steps, j), ta=True)


def f32(*shape):
    return pltpu.VMEM(shape, F32)


def out(dtype, *shape):
    return jax.ShapeDtypeStruct(shape, dtype)


def call(body, ins, outs, scratch=(), hbm=(), after=(), flops=1000, shared={}):
    names = [name for name in ins]
    flat, tree = jax.tree.flatten([ins[name] for name in names])
    outs = dict(outs)
    flat_outs, out_tree = jax.tree.flatten(outs)
    specs = jax.tree.leaves(
        [
            jax.tree.map(
                lambda _: pl.BlockSpec(memory_space=pltpu.HBM if name in hbm else pltpu.VMEM),
                ins[name],
            )
            for name in names
        ]
    )
    after = list(after)

    def kernel(*refs):
        values = jax.tree.unflatten(tree, refs[: len(flat)])
        start = len(flat) + len(after)
        results = jax.tree.unflatten(out_tree, refs[start : start + len(flat_outs)])
        results.update({name: results[old] for name, old in shared.items()})
        body(
            types.SimpleNamespace(**dict(zip(names, values))),
            types.SimpleNamespace(**results),
            *refs[start + len(flat_outs) :],
        )

    results = pl.pallas_call(
        kernel,
        out_shape=flat_outs,
        in_specs=specs + [pl.BlockSpec(memory_space=pl.ANY)] * len(after),
        scratch_shapes=[pltpu.VMEM(s, F32) if isinstance(s, tuple) else s for s in scratch],
        compiler_params=pltpu.CompilerParams(vmem_limit_bytes=16 * 1024 * 1024),
        cost_estimate=pl.CostEstimate(flops=flops, bytes_accessed=0, transcendentals=0),
    )(*flat, *after)
    return types.SimpleNamespace(**jax.tree.unflatten(out_tree, results))


def swap(piece, i):
    return lax.ppermute(piece, "seq", [(d, d ^ i) for d in range(lax.axis_size("seq"))])


def local(queries, keys, values, betas, gain, out_grad):
    tokens, heads, dim = queries.shape
    substeps = keys.shape[1]
    steps = tokens * substeps
    group = GROUP
    count = lax.axis_size("seq")
    groups = count // group
    two = groups == 2
    bind = functools.partial
    q2 = queries.reshape(tokens * heads, dim)
    g2 = out_grad.reshape(tokens * heads, dim)
    k2 = keys.reshape(steps * heads, dim)
    v2 = values.reshape(steps * heads, dim)
    packed = betas.transpose(1, 2, 0).reshape(substeps * heads, tokens)

    def chunk_outs(width):
        return dict(
            maps=[f32(dim, width) for _ in SOONER],
            unit=f32(2, steps, dim),
            inverse=f32(2, steps, steps),
            w=f32(2, steps, dim),
            e=f32(2, steps, dim),
        )

    read_outs = dict(q_unit=f32(2, tokens, dim), scores=f32(2, tokens, steps))
    a = call(
        bind(first_kernel, group, SOONER),
        {
            name: pltpu.with_memory_space_constraint(x, pltpu.HBM)
            for name, x in (
                ("k", k2),
                ("v", v2),
                ("q", q2),
                ("og", g2),
                ("packed", packed),
                ("gain", gain.reshape(1, dim)),
            )
        },
        dict(
            chunk_outs(5 * dim),
            **read_outs,
            rates=f32(steps, heads),
            rows=f32(heads, steps),
            kf=f32(steps * heads, dim),
            vf=f32(steps * heads, dim),
            qf=f32(tokens * heads, dim),
            gf=f32(tokens * heads, dim),
            gain=f32(1, dim),
        ),
        scratch=[pltpu.VMEM((steps * heads, dim), BF16)] * 2
        + [pltpu.VMEM((tokens * heads, dim), BF16)] * 2
        + [(substeps * heads, tokens), pltpu.SemaphoreType.DMA((6,))],
        hbm=("k", "v", "q", "og", "packed", "gain"),
        shared=dict(reads="maps"),
    )
    got = {h: swap(a.maps[i], h) for i, h in enumerate(SOONER)}
    b = call(
        bind(next_kernel, group, LATER),
        dict(kf=a.kf, vf=a.vf, rates=a.rates, rows=a.rows),
        chunk_outs(2 * dim),
    )
    for i, h in enumerate(LATER):
        got[h] = swap(b.maps[i], h) if h else b.maps[i]
    unit, inverse, w, e = (
        [getattr(x, name) for x in (a, b)] for name in ("unit", "inverse", "w", "e")
    )
    rates = a.rates
    c = call(
        bind(second_kernel, group, LATER),
        dict(qf=a.qf, gf=a.gf, rates=rates, unit=unit, inverse=inverse, w=w, e=e),
        dict(read_outs, reads=[f32(tokens, 3 * dim)] * 2, kx=f32(heads, steps, dim)),
        after=[got[SOONER[0]]],
        flops=10**9,
    )
    q_unit, scores = [a.q_unit, c.q_unit], [a.scores, c.scores]
    own_reads, got_reads = {}, {}
    for i in range(2):
        own_reads[SOONER[i]], own_reads[LATER[i]] = a.maps[i], c.reads[i]
        got_reads[SOONER[i]] = got[SOONER[i]]
        got_reads[LATER[i]] = swap(c.reads[i], LATER[i]) if LATER[i] else c.reads[i]
    own_reads, got_reads = ([x[h] for h in range(heads)] for x in (own_reads, got_reads))
    j = call(
        bind(join_kernel, group),
        dict(maps=[got[h] for h in range(heads)]),
        dict(
            starts=f32(group, dim, dim), total=f32(dim, dim), maps=f32(group, dim, 2 * dim)
        ),
        after=[c.kx],
    )
    ahead = [(d, d + group) for d in range(count - group)]
    behind = [(d + group, d) for d in range(count - group)]
    across = [(d, d ^ group) for d in range(count)]
    entry = lax.ppermute(j.total, "seq", across if two else ahead)
    p = call(
        bind(products_kernel, group),
        dict(maps=j.maps),
        dict(before=f32(group + 1, dim, dim), after=f32(group, dim, dim)),
    )
    for _ in range(groups - 2):
        passed = jnp.dot(p.before[group], entry, precision=lax.Precision.HIGHEST) + j.total
        entry = lax.ppermute(passed, "seq", ahead)
    own = call(
        bind(owner_kernel, group, 1 if two else None),
        dict(
            entry=entry,
            reads=got_reads,
            gain=a.gain,
            maps=j.maps,
            before=p.before,
            starts=j.starts,
        ),
        dict(
            starts=f32(group, dim, dim),
            entries=f32(group, dim, dim),
            total=f32(dim + 8, dim),
            states=[f32(dim + 8, dim)] * heads,
        ),
        scratch=[(group, tokens, 3 * dim)],
    )
    entry = lax.ppermute(own.total, "seq", across if two else behind)
    for _ in range(groups - 2):
        passed = jnp.dot(p.before[group].T, entry[:dim], precision=lax.Precision.HIGHEST)
        entry = lax.ppermute(own.total.at[:dim].add(passed), "seq", behind)
    states = [own.states[0]] + [swap(own.states[h], h) for h in range(1, heads)]
    adjoints = call(
        bind(spread_kernel, group, 0 if two else None),
        dict(entry=entry, starts=own.starts, maps=p.after),
        dict(adjoints=[f32(dim + 8, dim)] * heads),
    ).adjoints
    first_adjoint = adjoints[0]
    adjoints = [adjoints[0]] + [swap(adjoints[h], h) for h in range(1, heads)]
    t = call(
        bind(tokens_kernel, group),
        dict(
            states=states,
            reads=own_reads,
            gain=a.gain,
            qf=a.qf,
            rates=rates,
            w=w,
            e=e,
            q_unit=q_unit,
            unit=unit,
            scores=scores,
            inverse=inverse,
        ),
        dict(
            normed=out(BF16, tokens * heads, dim),
            dq=out(BF16, tokens * heads, dim),
            err=f32(heads, steps, dim),
            dk=f32(heads, steps, dim),
            z=f32(heads, steps, dim),
        ),
        scratch=[(tokens * heads, dim)] * 2,
        after=[first_adjoint],
    )
    sums = call(
        gain_kernel, dict(states=states, adjoints=adjoints), dict(gain=f32(1, dim)), after=[t.err]
    ).gain
    size = lax.axis_size("head")
    last = call(
        bind(last_kernel, group),
        dict(
            kf=a.kf,
            rates=rates,
            unit=unit,
            err=t.err,
            kx=c.kx,
            z=t.z,
            dk=t.dk,
            adjoints=adjoints,
            states=states,
        ),
        dict(
            dk=out(BF16, steps * heads, dim),
            dv=out(BF16, steps * heads, dim),
            db=out(F32, substeps * heads, tokens),
        ),
        scratch=[(steps * heads, dim)] * 2,
        after=[sums],
    )
    if two:
        gain_sum = sums + sum(
            lax.ppermute(sums, "head", [(d, d ^ flip) for d in range(size)])
            for flip in range(1, size)
        )
    else:
        gain_sum = lax.psum(own.total[dim:][:1], ("seq", "head"))
    return (
        t.normed.reshape(tokens, heads, dim),
        t.dq.reshape(tokens, heads, dim),
        last.dk.reshape(tokens, substeps, heads, dim),
        last.dv.reshape(tokens, substeps, heads, dim),
        last.db.reshape(substeps, heads, tokens).transpose(2, 0, 1),
        gain_sum.reshape(dim),
    )


def solution(mesh):
    return jax.shard_map(
        local,
        mesh=mesh,
        in_specs=(
            P("seq", "head", None),
            P("seq", None, "head", None),
            P("seq", None, "head", None),
            P("seq", None, "head"),
            P(),
            P("seq", "head", None),
        ),
        out_specs=(
            P("seq", "head", None),
            P("seq", "head", None),
            P("seq", None, "head", None),
            P("seq", None, "head", None),
            P("seq", None, "head"),
            P(),
        ),
        check_vma=False,
    )
```

```python
import functools
import types

import jax
import jax.numpy as jnp
from jax import lax
from jax.experimental import pallas as pl
from jax.experimental.pallas import tpu as pltpu
from jax.sharding import PartitionSpec as P

EPS = 1e-06
GROUP = 4
HALF = 128
BASE = 16
F32 = jnp.float32
BF16 = jnp.bfloat16


def split(x):
    high = x.astype(BF16)
    return high, (x - high.astype(F32)).astype(BF16)


def mm(a, b, ta=False, tb=False):
    (ah, al), (bh, bl) = split(a), split(b)
    if ta:
        ah, al = ah.T, al.T
    dims = (((1,), (1 if tb else 0,)), ((), ()))
    if b.shape[0 if tb else 1] > 128:
        left = jnp.concatenate([ah, ah, al], axis=1)
        right = jnp.concatenate([bh, bl, bh], axis=1 if tb else 0)
        return lax.dot_general(left, right, dims, preferred_element_type=F32)
    left = jnp.concatenate([ah, al], axis=1)
    if tb:
        right = jnp.concatenate(
            [jnp.concatenate([bh, bh], axis=1), jnp.concatenate([bl, bl], axis=1)], axis=0
        )
        width = b.shape[0]
    else:
        right = jnp.concatenate([bh, bl], axis=1)
        right = jnp.concatenate([right, right], axis=0)
        width = b.shape[1]
    both = lax.dot_general(left, right, dims, preferred_element_type=F32)
    return both[:, :width] + both[:, width:]


def exact_nt(a, b):
    return lax.dot_general(a, b, (((1,), (1,)), ((), ())), preferred_element_type=F32)


def iota(shape, dim):
    return lax.broadcasted_iota(jnp.int32, shape, dim)


def row_of(column):
    square = jnp.where(iota((HALF, HALF), 0) == iota((HALF, HALF), 1), column, 0.0)
    return jnp.sum(square, axis=0, keepdims=True)


def places(steps, j):
    shape = (steps, steps // 2)
    return (iota(shape, 0) == 2 * iota(shape, 1) + j).astype(F32)


def pick(a, b, ta=False, tb=False):
    dims = (((0 if ta else 1,), (1 if tb else 0,)), ((), ()))
    return lax.dot_general(
        a, b, dims, precision=lax.Precision.HIGHEST, preferred_element_type=F32
    )


def rate_column(rates, head):
    return jnp.sum(jnp.where(iota(rates.shape, 1) == head, rates, 0.0), axis=1, keepdims=True)


def small_inverses(lowers, rate_rows):
    blocks = HALF // BASE
    lane = iota((BASE, HALF), 1)
    row = iota((BASE, HALF), 0)
    jobs = range(len(lowers))
    packed = []
    for lower in lowers:
        one = lower[:BASE]
        for b in range(1, blocks):
            one = jnp.where(lane // BASE == b, lower[b * BASE : (b + 1) * BASE], one)
        packed.append(one)
    scaled = [packed[n] * rate_rows[n] for n in jobs]
    for j in range(BASE - 1):
        index = lane // BASE * BASE + j
        factors = [
            jnp.take_along_axis(scaled[n], index, axis=1, mode="promise_in_bounds") for n in jobs
        ]
        packed = [
            packed[n] - jnp.where(row > j, factors[n], 0.0) * packed[n][j : j + 1] for n in jobs
        ]
    return [
        jnp.concatenate(
            [jnp.where(lane // BASE == b, one, 0.0) for b in range(blocks)], axis=0
        )
        for one in packed
    ]


def place_in(group):
    return lax.rem(lax.axis_index("seq"), group)


def strided(ref, head, rows):
    return ref[pl.ds(head, rows, stride=ref.shape[0] // rows), :]


def store_strided(ref, head, value):
    rows = value.shape[0]
    ref[pl.ds(head, rows, stride=ref.shape[0] // rows), :] = value


SOONER, LATER = (1, 2), (3, 0)


def take(pairs, heads):
    order = SOONER + LATER
    return [pairs[order.index(h) // 2][order.index(h) % 2] for h in heads]


def inverse_norm(rows):
    return lax.rsqrt(jnp.sum(rows * rows, axis=1, keepdims=True) + EPS)


def unit_grad(inv, unit, grad):
    return inv * (grad - unit * jnp.sum(unit * grad, axis=1, keepdims=True))


def chunk(me, heads, kf, vf, rates, rows, o, wait):
    steps = rates.shape[0]
    strict = iota((HALF, HALF), 1) < iota((HALF, HALF), 0)
    rate = [rate_column(rates, me ^ h) for h in heads]
    rate_rows = [rows[pl.ds(me ^ h, 1), :] for h in heads]
    sides = [slice(0, HALF), slice(HALF, 2 * HALF)]
    raws = [strided(kf, me ^ h, steps) for h in heads]
    heads = range(len(heads)) if wait is None else heads
    count = range(len(raws))
    invs = [inverse_norm(raw) for raw in raws]
    inv_rows = [[row_of(inv[side]) for side in sides] for inv in invs]
    units = [raw * inv for raw, inv in zip(raws, invs)]
    raw16 = [raw.astype(BF16) for raw in raws]
    jobs = [(i, b) for i in count for b in range(2)]
    diag = {
        (i, b): jnp.where(
            strict,
            exact_nt(raw16[i][sides[b]], raw16[i][sides[b]]) * invs[i][sides[b]] * inv_rows[i][b],
            0.0,
        )
        for i, b in jobs
    }
    cross = [
        exact_nt(raw16[i][sides[1]], raw16[i][sides[0]]) * invs[i][sides[1]] * inv_rows[i][0]
        for i in count
    ]
    across = {(i, b): rate_rows[i][:, sides[b]] for i, b in jobs}
    inverse = dict(zip(jobs, small_inverses([diag[n] for n in jobs], [across[n] for n in jobs])))
    size = BASE
    while size < HALF:
        r, c = iota((HALF, HALF), 0) // size, iota((HALF, HALF), 1) // size
        below = (r % 2 == 1) & (c == r - 1)
        part = {n: jnp.where(below, diag[n], 0.0) for n in jobs}
        right = {n: part[n] - mm(part[n] * across[n], inverse[n]) for n in jobs}
        inverse = {
            n: inverse[n] + right[n] - mm(inverse[n] * across[n], right[n]) for n in jobs
        }
        size *= 2
    right = [cross[i] - mm(cross[i] * across[i, 0], inverse[i, 0]) for i in count]
    joined = [right[i] - mm(inverse[i, 1] * across[i, 1], right[i]) for i in count]
    vals = vf()
    both = [jnp.concatenate([units[i], vals[i]], axis=1) for i in count]
    top = [both[i][:HALF] - mm(inverse[i, 0] * across[i, 0], both[i][:HALF]) for i in count]
    low = [
        jnp.concatenate([joined[i] * across[i, 0], inverse[i, 1] * across[i, 1]], axis=1)
        for i in count
    ]
    bottom = [both[i][HALF:] - mm(low[i], both[i]) for i in count]
    solved = [jnp.concatenate([top[i], bottom[i]], axis=0) for i in count]
    eye = (iota((HALF, 2 * HALF), 0) == iota((HALF, 2 * HALF), 1)).astype(F32)
    sign = jnp.where(iota((HALF, 2 * HALF), 1) < HALF, -1.0, 1.0)
    ends = [eye + sign * mm(units[i], rate[i] * solved[i], ta=True) for i in count]
    for i in count:
        o.maps[i][:, : 2 * HALF] = ends[i]
        o.unit[i] = units[i]
        o.inverse[i, :HALF, :HALF] = inverse[i, 0]
        o.inverse[i, :HALF, HALF:] = jnp.zeros((HALF, HALF), F32)
        o.inverse[i, HALF:, :HALF] = joined[i]
        o.inverse[i, HALF:, HALF:] = inverse[i, 1]
        o.w[i] = solved[i][:, :HALF]
        o.e[i] = solved[i][:, HALF:]
    return units, [x[:, :HALF] for x in solved], [x[:, HALF:] for x in solved]


def first_kernel(group, heads, n, o, k16, v16, q16, g16, p32, sems):
    copies = [
        pltpu.make_async_copy(src, dst, sems.at[c])
        for c, (src, dst) in enumerate(
            (
                (n.packed, p32),
                (n.k, k16),
                (n.v, v16),
                (n.q, q16),
                (n.og, g16),
                (n.gain, o.gain),
            )
        )
    ]
    for copy in copies:
        copy.start()
    me = place_in(group)
    steps, count = o.rates.shape
    copies[0].wait()
    packed = p32[...]
    own, place = [packed[:count], packed[count:]], [places(steps, j) for j in range(2)]
    rates = pick(place[0], own[0], tb=True) + pick(place[1], own[1], tb=True)
    o.rates[...] = rates
    o.rows[...] = pick(own[0], place[0], tb=True) + pick(own[1], place[1], tb=True)
    copies[1].wait()
    o.kf[...] = k16[...].astype(F32)
    copies[2].wait()
    o.vf[...] = v16[...].astype(F32)
    for copy in copies[3:]:
        copy.wait()
    o.qf[...] = q16[...].astype(F32)
    o.gf[...] = g16[...].astype(F32)
    tokens = steps // 2
    vals = [strided(o.vf, me ^ h, steps) for h in heads]
    qs = [strided(o.qf, me ^ h, tokens) for h in heads]
    given = [strided(o.gf, me ^ h, tokens) for h in heads]
    solved = chunk(me, heads, o.kf, lambda: vals, rates, o.rows, o, None)
    reads(heads, qs, given, rates, *solved, me, o)


def next_kernel(group, heads, n, o):
    me = place_in(group)
    steps = n.rates.shape[0]
    vals = [strided(n.vf, me ^ h, steps) for h in heads]
    chunk(me, heads, n.kf, lambda: vals, n.rates[...], n.rows, o, None)


def reads(heads, qs, given, rates, keys, w, e, me, o):
    tokens = qs[0].shape[0]
    steps = 2 * tokens
    count = range(len(heads))
    seen = iota((tokens, steps), 1) <= 2 * iota((tokens, steps), 0) + 1
    rate = [rate_column(rates, me ^ h) for h in heads]
    weighted = [rate[i] * jnp.concatenate([w[i], e[i]], axis=1) for i in count]
    units = [q * inverse_norm(q) for q in qs]
    scores = [jnp.where(seen, mm(units[i], keys[i], tb=True), 0.0) for i in count]
    rows = [mm(scores[i], weighted[i]) for i in count]
    for i in count:
        o.q_unit[i] = units[i]
        o.scores[i] = scores[i]
        out = o.reads[i]
        skip = out.shape[1] - 3 * HALF
        out[:, skip : skip + HALF] = units[i] - rows[i][:, :HALF]
        out[:, skip + HALF : skip + 2 * HALF] = rows[i][:, HALF:]
        out[:, skip + 2 * HALF :] = given[i]


def second_kernel(group, heads, n, o):
    me = place_in(group)
    tokens = o.scores.shape[1]
    rates = n.rates[...]
    qs = [strided(n.qf, me ^ h, tokens) for h in heads]
    given = [strided(n.gf, me ^ h, tokens) for h in heads]
    keys, w, e = (take(x, heads) for x in (n.unit, n.w, n.e))
    every = range(o.kx.shape[0])
    rate = [rate_column(rates, me ^ i) for i in every]
    units, inverse = (take(x, every) for x in (n.unit, n.inverse))
    spread = [units[i] - mm(inverse[i], rate[i] * units[i], ta=True) for i in every]
    reads(heads, qs, given, rates, keys, w, e, me, o)
    for i in every:
        o.kx[i] = spread[i]


def join_kernel(group, n, o):
    me = place_in(group)
    for i, piece in enumerate(n.maps):
        o.maps[me ^ i] = piece[:, : 2 * HALF]
    state = jnp.zeros((HALF, HALF), F32)
    for j in range(group):
        o.starts[j] = state
        own = o.maps[j, :, HALF:]
        state = own if j == 0 else mm(o.maps[j, :, :HALF], state) + own
    o.total[...] = state


def products_kernel(group, n, o):
    eye = (iota((HALF, HALF), 0) == iota((HALF, HALF), 1)).astype(F32)
    steps = [n.maps[j, :, :HALF] for j in range(group)]
    before, after = [eye, steps[0]], [eye, steps[-1]]
    for j in range(1, group):
        before.append(mm(steps[j], before[-1]))
        after.append(mm(after[-1], steps[-1 - j]))
    o.middle[...] = mm(steps[2], steps[1])
    for j in range(group + 1):
        o.before[j] = before[j]
    for j in range(group):
        o.after[j] = after[group - 1 - j]


def spread_kernel(group, side, n, o):
    me = place_in(group)
    entry = n.entry[:HALF, :]
    if side is not None:
        entry = jnp.where(lax.axis_index("seq") // group == side, entry, 0.0)
    starts = [n.starts[me ^ i] for i in range(group)]
    maps = [n.maps[me ^ i] for i in range(group)]
    values = [starts[i] + mm(maps[i], entry, ta=True) for i in range(group)]
    for i, out in enumerate(o.adjoints):
        out[:HALF, :] = values[i]
        out[HALF:, :] = n.entry[HALF:, :]


def normed_and_grads(queries, parts, states, given, gain):
    count = range(len(queries))
    reads = [parts[i] + mm(queries[i], states[i]) for i in count]
    inv_rms = [lax.rsqrt(jnp.mean(read * read, axis=1, keepdims=True) + EPS) for read in reads]
    normal = [reads[i] * inv_rms[i] for i in count]
    scaled = [given[i] * gain for i in count]
    grads = [
        inv_rms[i] * (scaled[i] - normal[i] * jnp.mean(scaled[i] * normal[i], axis=1, keepdims=True))
        for i in count
    ]
    return normal, grads, sum(jnp.sum(given[i] * normal[i], axis=0, keepdims=True) for i in count)


def owner_kernel(group, side, n, o, packed):
    me = place_in(group)
    entry = n.entry[...]
    if side is not None:
        entry = jnp.where(lax.axis_index("seq") // group == side, entry, 0.0)
    for i, piece in enumerate(n.reads):
        packed[me ^ i] = piece[:, piece.shape[1] - 3 * HALF :]
    gain = n.gain[...]
    places_ = range(group)
    maps = [n.maps[j, :, :HALF] for j in places_]
    before = [n.before[j] for j in places_]
    starts = [n.starts[j] for j in places_]
    queries, parts, given = (
        [packed[j, :, c * HALF : (c + 1) * HALF] for j in places_] for c in range(3)
    )
    states = [starts[j] + mm(before[j], entry) if j else starts[j] + entry for j in places_]
    _, grads, gain_part = normed_and_grads(queries, parts, states, given, gain)
    adjoints = [mm(queries[j], grads[j], ta=True) for j in places_]
    chain = [
        adjoints[1] + mm(maps[1], adjoints[2], ta=True) + mm(n.middle[...], adjoints[3], ta=True),
        adjoints[2] + mm(maps[2], adjoints[3], ta=True),
        adjoints[3],
        jnp.zeros((HALF, HALF), F32),
    ]
    total = adjoints[0] + sum(mm(before[j], adjoints[j], ta=True) for j in range(1, group))
    for j in places_:
        o.starts[j] = chain[j]
        o.entries[j] = states[j]
    o.total[:HALF, :] = total
    for i in places_:
        o.states[i][:HALF, :] = o.entries[me ^ i]
        o.states[i][HALF:, :] = jnp.broadcast_to(gain_part, (8, HALF))
    o.total[HALF:, :] = jnp.broadcast_to(gain_part, (8, HALF))


def tokens_kernel(group, n, o, of, df):
    me = place_in(group)
    heads, tokens, steps = range(len(n.reads)), n.reads[0].shape[0], n.rates.shape[0]
    gain = n.gain[...]
    rates = n.rates[...]
    queries, parts, given = (
        [
            ref[:, ref.shape[1] - (3 - c) * HALF : ref.shape[1] - (2 - c) * HALF]
            for ref in n.reads
        ]
        for c in range(3)
    )
    states = [ref[:HALF, :] for ref in n.states]
    seen = iota((tokens, steps), 1) <= 2 * iota((tokens, steps), 0) + 1
    raws = [strided(n.qf, me ^ i, tokens) for i in heads]
    keys, w, e, units, inverse, scores = (
        take(x, heads) for x in (n.unit, n.w, n.e, n.q_unit, n.inverse, n.scores)
    )
    rate = [rate_column(rates, me ^ i) for i in heads]
    invs = [inverse_norm(raw) for raw in raws]
    errs = [e[i] - mm(w[i], states[i]) for i in heads]
    normal, grads, _ = normed_and_grads(queries, parts, states, given, gain)
    pseudo = [rate[i] * errs[i] for i in heads]
    d_scores = [jnp.where(seen, mm(grads[i], pseudo[i], tb=True), 0.0) for i in heads]
    d_pseudo = [mm(scores[i], grads[i], ta=True) for i in heads]
    d_units = [mm(grads[i], states[i], tb=True) + mm(d_scores[i], keys[i]) for i in heads]
    z = [d_pseudo[i] - mm(inverse[i], rate[i] * d_pseudo[i], ta=True) for i in heads]
    d_keys = [mm(d_scores[i], units[i], ta=True) for i in heads]
    done = [unit_grad(invs[i], units[i], d_units[i]) for i in heads]
    for i in heads:
        o.err[i] = errs[i]
        o.dk[i] = d_keys[i]
        o.z[i] = z[i]
        store_strided(of, me ^ i, gain * normal[i])
        store_strided(df, me ^ i, done[i])
    o.normed[...] = of[...].astype(BF16)
    o.dq[...] = df[...].astype(BF16)


def gain_kernel(n, o):
    o.gain[...] = sum(ref[HALF : HALF + 1, :] for ref in n.states + n.adjoints)


def last_kernel(group, n, o, df, vf):
    me = place_in(group)
    rates = n.rates[...]
    steps, count = rates.shape
    heads = range(count)
    rate = [rate_column(rates, me ^ i) for i in heads]
    raws = [strided(n.kf, me ^ i, steps) for i in heads]
    adjoints = [ref[:HALF, :] for ref in n.adjoints]
    states = [ref[:HALF, :] for ref in n.states]
    units = take(n.unit, heads)
    errs, kx, z0, dk0 = ([x[i] for i in heads] for x in (n.err, n.kx, n.z, n.dk))
    z = [z0[i] + mm(kx[i], adjoints[i]) for i in heads]
    invs = [inverse_norm(raw) for raw in raws]
    pseudo = [rate[i] * errs[i] for i in heads]
    d_values = [rate[i] * z[i] for i in heads]
    half = steps // 2
    below = iota((half, half), 1) < iota((half, half), 0)
    d_grams = []
    for i in heads:
        later = mm(d_values[i][half:], pseudo[i], tb=True)
        corners = [
            jnp.where(below, corner, 0.0)
            for corner in (mm(d_values[i][:half], pseudo[i][:half], tb=True), later[:, half:])
        ]
        corners = [corner + corner.T for corner in corners]
        d_grams.append(
            jnp.concatenate(
                [
                    jnp.concatenate([corners[0], later[:, :half].T], axis=1),
                    jnp.concatenate([later[:, :half], corners[1]], axis=1),
                ],
                axis=0,
            )
        )
    d_units = [
        dk0[i]
        + mm(
            jnp.concatenate([pseudo[i], d_values[i], d_grams[i]], axis=1),
            jnp.concatenate([adjoints[i].T, -states[i].T, -units[i]], axis=0),
        )
        for i in heads
    ]
    done = [unit_grad(invs[i], units[i], d_units[i]) for i in heads]
    d_rates = jnp.zeros(rates.shape, F32)
    for i in heads:
        d_rate = jnp.sum(z[i] * errs[i], axis=1, keepdims=True)
        d_rates = jnp.where(iota(rates.shape, 1) == me ^ i, d_rate, d_rates)
        store_strided(vf, me ^ i, d_values[i])
        store_strided(df, me ^ i, done[i])
    o.dk[...] = df[...].astype(BF16)
    o.dv[...] = vf[...].astype(BF16)
    for j in range(2):
        o.db[j * count : (j + 1) * count, :] = pick(d_rates, places(steps, j), ta=True)


def f32(*shape):
    return pltpu.VMEM(shape, F32)


def out(dtype, *shape):
    return jax.ShapeDtypeStruct(shape, dtype)


def call(body, ins, outs, scratch=(), hbm=(), after=(), flops=1000, shared={}):
    names = [name for name in ins]
    flat, tree = jax.tree.flatten([ins[name] for name in names])
    outs = dict(outs)
    flat_outs, out_tree = jax.tree.flatten(outs)
    specs = jax.tree.leaves(
        [
            jax.tree.map(
                lambda _: pl.BlockSpec(memory_space=pltpu.HBM if name in hbm else pltpu.VMEM),
                ins[name],
            )
            for name in names
        ]
    )
    after = list(after)

    def kernel(*refs):
        values = jax.tree.unflatten(tree, refs[: len(flat)])
        start = len(flat) + len(after)
        results = jax.tree.unflatten(out_tree, refs[start : start + len(flat_outs)])
        results.update({name: results[old] for name, old in shared.items()})
        body(
            types.SimpleNamespace(**dict(zip(names, values))),
            types.SimpleNamespace(**results),
            *refs[start + len(flat_outs) :],
        )

    results = pl.pallas_call(
        kernel,
        out_shape=flat_outs,
        in_specs=specs + [pl.BlockSpec(memory_space=pl.ANY)] * len(after),
        scratch_shapes=[pltpu.VMEM(s, F32) if isinstance(s, tuple) else s for s in scratch],
        compiler_params=pltpu.CompilerParams(vmem_limit_bytes=16 * 1024 * 1024),
        cost_estimate=pl.CostEstimate(flops=flops, bytes_accessed=0, transcendentals=0),
    )(*flat, *after)
    return types.SimpleNamespace(**jax.tree.unflatten(out_tree, results))


def swap(piece, i):
    return lax.ppermute(piece, "seq", [(d, d ^ i) for d in range(lax.axis_size("seq"))])


def local(queries, keys, values, betas, gain, out_grad):
    tokens, heads, dim = queries.shape
    substeps = keys.shape[1]
    steps = tokens * substeps
    group = GROUP
    count = lax.axis_size("seq")
    groups = count // group
    two = groups == 2
    bind = functools.partial
    q2 = queries.reshape(tokens * heads, dim)
    g2 = out_grad.reshape(tokens * heads, dim)
    k2 = keys.reshape(steps * heads, dim)
    v2 = values.reshape(steps * heads, dim)
    packed = betas.transpose(1, 2, 0).reshape(substeps * heads, tokens)

    def chunk_outs(width):
        return dict(
            maps=[f32(dim, width) for _ in SOONER],
            unit=f32(2, steps, dim),
            inverse=f32(2, steps, steps),
            w=f32(2, steps, dim),
            e=f32(2, steps, dim),
        )

    read_outs = dict(q_unit=f32(2, tokens, dim), scores=f32(2, tokens, steps))
    a = call(
        bind(first_kernel, group, SOONER),
        {
            name: pltpu.with_memory_space_constraint(x, pltpu.HBM)
            for name, x in (
                ("k", k2),
                ("v", v2),
                ("q", q2),
                ("og", g2),
                ("packed", packed),
                ("gain", gain.reshape(1, dim)),
            )
        },
        dict(
            chunk_outs(5 * dim),
            **read_outs,
            rates=f32(steps, heads),
            rows=f32(heads, steps),
            kf=f32(steps * heads, dim),
            vf=f32(steps * heads, dim),
            qf=f32(tokens * heads, dim),
            gf=f32(tokens * heads, dim),
            gain=f32(1, dim),
        ),
        scratch=[pltpu.VMEM((steps * heads, dim), BF16)] * 2
        + [pltpu.VMEM((tokens * heads, dim), BF16)] * 2
        + [(substeps * heads, tokens), pltpu.SemaphoreType.DMA((6,))],
        hbm=("k", "v", "q", "og", "packed", "gain"),
        shared=dict(reads="maps"),
    )
    got = {h: swap(a.maps[i], h) for i, h in enumerate(SOONER)}
    b = call(
        bind(next_kernel, group, LATER),
        dict(kf=a.kf, vf=a.vf, rates=a.rates, rows=a.rows),
        chunk_outs(2 * dim),
    )
    for i, h in enumerate(LATER):
        got[h] = swap(b.maps[i], h) if h else b.maps[i]
    unit, inverse, w, e = (
        [getattr(x, name) for x in (a, b)] for name in ("unit", "inverse", "w", "e")
    )
    rates = a.rates
    c = call(
        bind(second_kernel, group, LATER),
        dict(qf=a.qf, gf=a.gf, rates=rates, unit=unit, inverse=inverse, w=w, e=e),
        dict(read_outs, reads=[f32(tokens, 3 * dim)] * 2, kx=f32(heads, steps, dim)),
        after=[got[SOONER[0]]],
        flops=10**9,
    )
    q_unit, scores = [a.q_unit, c.q_unit], [a.scores, c.scores]
    own_reads, got_reads = {}, {}
    for i in range(2):
        own_reads[SOONER[i]], own_reads[LATER[i]] = a.maps[i], c.reads[i]
        got_reads[SOONER[i]] = got[SOONER[i]]
        got_reads[LATER[i]] = swap(c.reads[i], LATER[i]) if LATER[i] else c.reads[i]
    own_reads, got_reads = ([x[h] for h in range(heads)] for x in (own_reads, got_reads))
    j = call(
        bind(join_kernel, group),
        dict(maps=[got[h] for h in range(heads)]),
        dict(
            starts=f32(group, dim, dim), total=f32(dim, dim), maps=f32(group, dim, 2 * dim)
        ),
        after=[c.kx],
    )
    ahead = [(d, d + group) for d in range(count - group)]
    behind = [(d + group, d) for d in range(count - group)]
    across = [(d, d ^ group) for d in range(count)]
    entry = lax.ppermute(j.total, "seq", across if two else ahead)
    p = call(
        bind(products_kernel, group),
        dict(maps=j.maps),
        dict(
            before=f32(group + 1, dim, dim),
            after=f32(group, dim, dim),
            middle=f32(dim, dim),
        ),
    )
    for _ in range(groups - 2):
        passed = jnp.dot(p.before[group], entry, precision=lax.Precision.HIGHEST) + j.total
        entry = lax.ppermute(passed, "seq", ahead)
    own = call(
        bind(owner_kernel, group, 1 if two else None),
        dict(
            entry=entry,
            reads=got_reads,
            gain=a.gain,
            maps=j.maps,
            before=p.before,
            middle=p.middle,
            starts=j.starts,
        ),
        dict(
            starts=f32(group, dim, dim),
            entries=f32(group, dim, dim),
            total=f32(dim + 8, dim),
            states=[f32(dim + 8, dim)] * heads,
        ),
        scratch=[(group, tokens, 3 * dim)],
    )
    entry = lax.ppermute(own.total, "seq", across if two else behind)
    for _ in range(groups - 2):
        passed = jnp.dot(p.before[group].T, entry[:dim], precision=lax.Precision.HIGHEST)
        entry = lax.ppermute(own.total.at[:dim].add(passed), "seq", behind)
    states = [own.states[0]] + [swap(own.states[h], h) for h in range(1, heads)]
    adjoints = call(
        bind(spread_kernel, group, 0 if two else None),
        dict(entry=entry, starts=own.starts, maps=p.after),
        dict(adjoints=[f32(dim + 8, dim)] * heads),
    ).adjoints
    first_adjoint = adjoints[0]
    adjoints = [adjoints[0]] + [swap(adjoints[h], h) for h in range(1, heads)]
    t = call(
        bind(tokens_kernel, group),
        dict(
            states=states,
            reads=own_reads,
            gain=a.gain,
            qf=a.qf,
            rates=rates,
            w=w,
            e=e,
            q_unit=q_unit,
            unit=unit,
            scores=scores,
            inverse=inverse,
        ),
        dict(
            normed=out(BF16, tokens * heads, dim),
            dq=out(BF16, tokens * heads, dim),
            err=f32(heads, steps, dim),
            dk=f32(heads, steps, dim),
            z=f32(heads, steps, dim),
        ),
        scratch=[(tokens * heads, dim)] * 2,
        after=[first_adjoint],
    )
    sums = call(
        gain_kernel, dict(states=states, adjoints=adjoints), dict(gain=f32(1, dim)), after=[t.err]
    ).gain
    size = lax.axis_size("head")
    last = call(
        bind(last_kernel, group),
        dict(
            kf=a.kf,
            rates=rates,
            unit=unit,
            err=t.err,
            kx=c.kx,
            z=t.z,
            dk=t.dk,
            adjoints=adjoints,
            states=states,
        ),
        dict(
            dk=out(BF16, steps * heads, dim),
            dv=out(BF16, steps * heads, dim),
            db=out(F32, substeps * heads, tokens),
        ),
        scratch=[(steps * heads, dim)] * 2,
        after=[sums],
    )
    if two:
        gain_sum = sums + sum(
            lax.ppermute(sums, "head", [(d, d ^ flip) for d in range(size)])
            for flip in range(1, size)
        )
    else:
        gain_sum = lax.psum(own.total[dim:][:1], ("seq", "head"))
    return (
        t.normed.reshape(tokens, heads, dim),
        t.dq.reshape(tokens, heads, dim),
        last.dk.reshape(tokens, substeps, heads, dim),
        last.dv.reshape(tokens, substeps, heads, dim),
        last.db.reshape(substeps, heads, tokens).transpose(2, 0, 1),
        gain_sum.reshape(dim),
    )


def solution(mesh):
    return jax.shard_map(
        local,
        mesh=mesh,
        in_specs=(
            P("seq", "head", None),
            P("seq", None, "head", None),
            P("seq", None, "head", None),
            P("seq", None, "head"),
            P(),
            P("seq", "head", None),
        ),
        out_specs=(
            P("seq", "head", None),
            P("seq", "head", None),
            P("seq", None, "head", None),
            P("seq", None, "head", None),
            P("seq", None, "head"),
            P(),
        ),
        check_vma=False,
    )
```

```python
import functools
import types

import jax
import jax.numpy as jnp
from jax import lax
from jax.experimental import pallas as pl
from jax.experimental.pallas import tpu as pltpu
from jax.sharding import PartitionSpec as P

EPS = 1e-06
GROUP = 4
HALF = 128
BASE = 16
F32 = jnp.float32
BF16 = jnp.bfloat16


def split(x):
    high = x.astype(BF16)
    return high, (x - high.astype(F32)).astype(BF16)


def mm(a, b, ta=False, tb=False):
    (ah, al), (bh, bl) = split(a), split(b)
    if ta:
        ah, al = ah.T, al.T
    dims = (((1,), (1 if tb else 0,)), ((), ()))
    if b.shape[0 if tb else 1] > 128:
        left = jnp.concatenate([ah, ah, al], axis=1)
        right = jnp.concatenate([bh, bl, bh], axis=1 if tb else 0)
        return lax.dot_general(left, right, dims, preferred_element_type=F32)
    left = jnp.concatenate([ah, al], axis=1)
    if tb:
        right = jnp.concatenate(
            [jnp.concatenate([bh, bh], axis=1), jnp.concatenate([bl, bl], axis=1)], axis=0
        )
        width = b.shape[0]
    else:
        right = jnp.concatenate([bh, bl], axis=1)
        right = jnp.concatenate([right, right], axis=0)
        width = b.shape[1]
    both = lax.dot_general(left, right, dims, preferred_element_type=F32)
    return both[:, :width] + both[:, width:]


def exact_nt(a, b):
    return lax.dot_general(a, b, (((1,), (1,)), ((), ())), preferred_element_type=F32)


def iota(shape, dim):
    return lax.broadcasted_iota(jnp.int32, shape, dim)


def row_of(column):
    square = jnp.where(iota((HALF, HALF), 0) == iota((HALF, HALF), 1), column, 0.0)
    return jnp.sum(square, axis=0, keepdims=True)


def places(steps, j):
    shape = (steps, steps // 2)
    return (iota(shape, 0) == 2 * iota(shape, 1) + j).astype(F32)


def pick(a, b, ta=False, tb=False):
    dims = (((0 if ta else 1,), (1 if tb else 0,)), ((), ()))
    return lax.dot_general(
        a, b, dims, precision=lax.Precision.HIGHEST, preferred_element_type=F32
    )


def rate_column(rates, head):
    return jnp.sum(jnp.where(iota(rates.shape, 1) == head, rates, 0.0), axis=1, keepdims=True)


def small_inverses(lowers, rate_rows):
    blocks = HALF // BASE
    lane = iota((BASE, HALF), 1)
    row = iota((BASE, HALF), 0)
    jobs = range(len(lowers))
    packed = []
    for lower in lowers:
        one = lower[:BASE]
        for b in range(1, blocks):
            one = jnp.where(lane // BASE == b, lower[b * BASE : (b + 1) * BASE], one)
        packed.append(one)
    scaled = [packed[n] * rate_rows[n] for n in jobs]
    for j in range(BASE - 1):
        index = lane // BASE * BASE + j
        factors = [
            jnp.take_along_axis(scaled[n], index, axis=1, mode="promise_in_bounds") for n in jobs
        ]
        packed = [
            packed[n] - jnp.where(row > j, factors[n], 0.0) * packed[n][j : j + 1] for n in jobs
        ]
    return [
        jnp.concatenate(
            [jnp.where(lane // BASE == b, one, 0.0) for b in range(blocks)], axis=0
        )
        for one in packed
    ]


def place_in(group):
    return lax.rem(lax.axis_index("seq"), group)


def strided(ref, head, rows):
    return ref[pl.ds(head, rows, stride=ref.shape[0] // rows), :]


def store_strided(ref, head, value):
    rows = value.shape[0]
    ref[pl.ds(head, rows, stride=ref.shape[0] // rows), :] = value


SOONER, LATER = (2, 1), (3, 0)


def take(pairs, heads):
    order = SOONER + LATER
    return [pairs[order.index(h) // 2][order.index(h) % 2] for h in heads]


def inverse_norm(rows):
    return lax.rsqrt(jnp.sum(rows * rows, axis=1, keepdims=True) + EPS)


def unit_grad(inv, unit, grad):
    return inv * (grad - unit * jnp.sum(unit * grad, axis=1, keepdims=True))


def chunk(me, heads, kf, vf, rates, rows, o, wait):
    steps = rates.shape[0]
    strict = iota((HALF, HALF), 1) < iota((HALF, HALF), 0)
    rate = [rate_column(rates, me ^ h) for h in heads]
    rate_rows = [rows[pl.ds(me ^ h, 1), :] for h in heads]
    sides = [slice(0, HALF), slice(HALF, 2 * HALF)]
    raws = [strided(kf, me ^ h, steps) for h in heads]
    heads = range(len(heads)) if wait is None else heads
    count = range(len(raws))
    invs = [inverse_norm(raw) for raw in raws]
    inv_rows = [[row_of(inv[side]) for side in sides] for inv in invs]
    units = [raw * inv for raw, inv in zip(raws, invs)]
    raw16 = [raw.astype(BF16) for raw in raws]
    jobs = [(i, b) for i in count for b in range(2)]
    diag = {
        (i, b): jnp.where(
            strict,
            exact_nt(raw16[i][sides[b]], raw16[i][sides[b]]) * invs[i][sides[b]] * inv_rows[i][b],
            0.0,
        )
        for i, b in jobs
    }
    cross = [
        exact_nt(raw16[i][sides[1]], raw16[i][sides[0]]) * invs[i][sides[1]] * inv_rows[i][0]
        for i in count
    ]
    across = {(i, b): rate_rows[i][:, sides[b]] for i, b in jobs}
    inverse = dict(zip(jobs, small_inverses([diag[n] for n in jobs], [across[n] for n in jobs])))
    size = BASE
    while size < HALF:
        r, c = iota((HALF, HALF), 0) // size, iota((HALF, HALF), 1) // size
        below = (r % 2 == 1) & (c == r - 1)
        part = {n: jnp.where(below, diag[n], 0.0) for n in jobs}
        right = {n: part[n] - mm(part[n] * across[n], inverse[n]) for n in jobs}
        inverse = {
            n: inverse[n] + right[n] - mm(inverse[n] * across[n], right[n]) for n in jobs
        }
        size *= 2
    right = [cross[i] - mm(cross[i] * across[i, 0], inverse[i, 0]) for i in count]
    joined = [right[i] - mm(inverse[i, 1] * across[i, 1], right[i]) for i in count]
    vals = vf()
    both = [jnp.concatenate([units[i], vals[i]], axis=1) for i in count]
    top = [both[i][:HALF] - mm(inverse[i, 0] * across[i, 0], both[i][:HALF]) for i in count]
    low = [
        jnp.concatenate([joined[i] * across[i, 0], inverse[i, 1] * across[i, 1]], axis=1)
        for i in count
    ]
    bottom = [both[i][HALF:] - mm(low[i], both[i]) for i in count]
    solved = [jnp.concatenate([top[i], bottom[i]], axis=0) for i in count]
    eye = (iota((HALF, 2 * HALF), 0) == iota((HALF, 2 * HALF), 1)).astype(F32)
    sign = jnp.where(iota((HALF, 2 * HALF), 1) < HALF, -1.0, 1.0)
    ends = [eye + sign * mm(units[i], rate[i] * solved[i], ta=True) for i in count]
    for i in count:
        o.maps[i][:, : 2 * HALF] = ends[i]
        o.unit[i] = units[i]
        o.inverse[i, :HALF, :HALF] = inverse[i, 0]
        o.inverse[i, :HALF, HALF:] = jnp.zeros((HALF, HALF), F32)
        o.inverse[i, HALF:, :HALF] = joined[i]
        o.inverse[i, HALF:, HALF:] = inverse[i, 1]
        o.w[i] = solved[i][:, :HALF]
        o.e[i] = solved[i][:, HALF:]
    return units, [x[:, :HALF] for x in solved], [x[:, HALF:] for x in solved]


def first_kernel(group, heads, n, o, k16, v16, q16, g16, p32, sems):
    copies = [
        pltpu.make_async_copy(src, dst, sems.at[c])
        for c, (src, dst) in enumerate(
            (
                (n.packed, p32),
                (n.k, k16),
                (n.v, v16),
                (n.q, q16),
                (n.og, g16),
                (n.gain, o.gain),
            )
        )
    ]
    for copy in copies:
        copy.start()
    me = place_in(group)
    steps, count = o.rates.shape
    copies[0].wait()
    packed = p32[...]
    own, place = [packed[:count], packed[count:]], [places(steps, j) for j in range(2)]
    rates = pick(place[0], own[0], tb=True) + pick(place[1], own[1], tb=True)
    o.rates[...] = rates
    o.rows[...] = pick(own[0], place[0], tb=True) + pick(own[1], place[1], tb=True)
    copies[1].wait()
    o.kf[...] = k16[...].astype(F32)
    copies[2].wait()
    o.vf[...] = v16[...].astype(F32)
    for copy in copies[3:]:
        copy.wait()
    o.qf[...] = q16[...].astype(F32)
    o.gf[...] = g16[...].astype(F32)
    tokens = steps // 2
    vals = [strided(o.vf, me ^ h, steps) for h in heads]
    qs = [strided(o.qf, me ^ h, tokens) for h in heads]
    given = [strided(o.gf, me ^ h, tokens) for h in heads]
    solved = chunk(me, heads, o.kf, lambda: vals, rates, o.rows, o, None)
    reads(heads, qs, given, rates, *solved, me, o, [o.maps[0], o.later_reads])


def next_kernel(group, heads, n, o):
    me = place_in(group)
    steps = n.rates.shape[0]
    vals = [strided(n.vf, me ^ h, steps) for h in heads]
    chunk(me, heads, n.kf, lambda: vals, n.rates[...], n.rows, o, None)


def reads(heads, qs, given, rates, keys, w, e, me, o, outs):
    tokens = qs[0].shape[0]
    steps = 2 * tokens
    count = range(len(heads))
    seen = iota((tokens, steps), 1) <= 2 * iota((tokens, steps), 0) + 1
    rate = [rate_column(rates, me ^ h) for h in heads]
    weighted = [rate[i] * jnp.concatenate([w[i], e[i]], axis=1) for i in count]
    units = [q * inverse_norm(q) for q in qs]
    scores = [jnp.where(seen, mm(units[i], keys[i], tb=True), 0.0) for i in count]
    rows = [mm(scores[i], weighted[i]) for i in count]
    for i in count:
        o.q_unit[i] = units[i]
        o.scores[i] = scores[i]
        out = outs[i]
        skip = out.shape[1] - 3 * HALF
        out[:, skip : skip + HALF] = units[i] - rows[i][:, :HALF]
        out[:, skip + HALF : skip + 2 * HALF] = rows[i][:, HALF:]
        out[:, skip + 2 * HALF :] = given[i]


def second_kernel(group, heads, n, o):
    me = place_in(group)
    tokens = o.scores.shape[1]
    rates = n.rates[...]
    qs = [strided(n.qf, me ^ h, tokens) for h in heads]
    given = [strided(n.gf, me ^ h, tokens) for h in heads]
    keys, w, e = (take(x, heads) for x in (n.unit, n.w, n.e))
    every = range(o.kx.shape[0])
    rate = [rate_column(rates, me ^ i) for i in every]
    units, inverse = (take(x, every) for x in (n.unit, n.inverse))
    spread = [units[i] - mm(inverse[i], rate[i] * units[i], ta=True) for i in every]
    reads(heads, qs, given, rates, keys, w, e, me, o, o.reads)
    for i in every:
        o.kx[i] = spread[i]


def hold_kernel(n, o):
    o.y[...] = n.x[...]


def join_kernel(group, n, o):
    me = place_in(group)
    for i, piece in enumerate(n.maps):
        o.maps[me ^ i] = piece[:, : 2 * HALF]
    state = jnp.zeros((HALF, HALF), F32)
    for j in range(group):
        o.starts[j] = state
        own = o.maps[j, :, HALF:]
        state = own if j == 0 else mm(o.maps[j, :, :HALF], state) + own
    o.total[...] = state


def products_kernel(group, n, o):
    eye = (iota((HALF, HALF), 0) == iota((HALF, HALF), 1)).astype(F32)
    steps = [n.maps[j, :, :HALF] for j in range(group)]
    before, after = [eye, steps[0]], [eye, steps[-1]]
    for j in range(1, group):
        before.append(mm(steps[j], before[-1]))
        after.append(mm(after[-1], steps[-1 - j]))
    o.middle[...] = mm(steps[2], steps[1])
    for j in range(group + 1):
        o.before[j] = before[j]
    for j in range(group):
        o.after[j] = after[group - 1 - j]


def spread_kernel(group, side, n, o):
    me = place_in(group)
    entry = n.entry[:HALF, :]
    if side is not None:
        entry = jnp.where(lax.axis_index("seq") // group == side, entry, 0.0)
    starts = [n.starts[me ^ i] for i in range(group)]
    maps = [n.maps[me ^ i] for i in range(group)]
    values = [starts[i] + mm(maps[i], entry, ta=True) for i in range(group)]
    for i, out in enumerate(o.adjoints):
        out[:HALF, :] = values[i]
        out[HALF:, :] = n.entry[HALF:, :]


def normed_and_grads(queries, parts, states, given, gain):
    count = range(len(queries))
    reads = [parts[i] + mm(queries[i], states[i]) for i in count]
    inv_rms = [lax.rsqrt(jnp.mean(read * read, axis=1, keepdims=True) + EPS) for read in reads]
    normal = [reads[i] * inv_rms[i] for i in count]
    scaled = [given[i] * gain for i in count]
    grads = [
        inv_rms[i] * (scaled[i] - normal[i] * jnp.mean(scaled[i] * normal[i], axis=1, keepdims=True))
        for i in count
    ]
    return normal, grads, sum(jnp.sum(given[i] * normal[i], axis=0, keepdims=True) for i in count)


def owner_kernel(group, side, n, o, packed):
    me = place_in(group)
    entry = n.entry[...]
    if side is not None:
        entry = jnp.where(lax.axis_index("seq") // group == side, entry, 0.0)
    for i, piece in enumerate(n.reads):
        packed[me ^ i] = piece[:, piece.shape[1] - 3 * HALF :]
    gain = n.gain[...]
    places_ = range(group)
    maps = [n.maps[j, :, :HALF] for j in places_]
    before = [n.before[j] for j in places_]
    starts = [n.starts[j] for j in places_]
    queries, parts, given = (
        [packed[j, :, c * HALF : (c + 1) * HALF] for j in places_] for c in range(3)
    )
    states = [starts[j] + mm(before[j], entry) if j else starts[j] + entry for j in places_]
    _, grads, gain_part = normed_and_grads(queries, parts, states, given, gain)
    adjoints = [mm(queries[j], grads[j], ta=True) for j in places_]
    chain = [
        adjoints[1] + mm(maps[1], adjoints[2], ta=True) + mm(n.middle[...], adjoints[3], ta=True),
        adjoints[2] + mm(maps[2], adjoints[3], ta=True),
        adjoints[3],
        jnp.zeros((HALF, HALF), F32),
    ]
    total = adjoints[0] + sum(mm(before[j], adjoints[j], ta=True) for j in range(1, group))
    for j in places_:
        o.starts[j] = chain[j]
        o.entries[j] = states[j]
    o.total[:HALF, :] = total
    for i in places_:
        o.states[i][:HALF, :] = o.entries[me ^ i]
        o.states[i][HALF:, :] = jnp.broadcast_to(gain_part, (8, HALF))
    o.total[HALF:, :] = jnp.broadcast_to(gain_part, (8, HALF))


def tokens_kernel(group, n, o, of, df):
    me = place_in(group)
    heads, tokens, steps = range(len(n.reads)), n.reads[0].shape[0], n.rates.shape[0]
    gain = n.gain[...]
    rates = n.rates[...]
    queries, parts, given = (
        [
            ref[:, ref.shape[1] - (3 - c) * HALF : ref.shape[1] - (2 - c) * HALF]
            for ref in n.reads
        ]
        for c in range(3)
    )
    states = [ref[:HALF, :] for ref in n.states]
    seen = iota((tokens, steps), 1) <= 2 * iota((tokens, steps), 0) + 1
    raws = [strided(n.qf, me ^ i, tokens) for i in heads]
    keys, w, e, units, inverse, scores = (
        take(x, heads) for x in (n.unit, n.w, n.e, n.q_unit, n.inverse, n.scores)
    )
    rate = [rate_column(rates, me ^ i) for i in heads]
    invs = [inverse_norm(raw) for raw in raws]
    errs = [e[i] - mm(w[i], states[i]) for i in heads]
    normal, grads, _ = normed_and_grads(queries, parts, states, given, gain)
    pseudo = [rate[i] * errs[i] for i in heads]
    d_scores = [jnp.where(seen, mm(grads[i], pseudo[i], tb=True), 0.0) for i in heads]
    d_pseudo = [mm(scores[i], grads[i], ta=True) for i in heads]
    d_units = [mm(grads[i], states[i], tb=True) + mm(d_scores[i], keys[i]) for i in heads]
    z = [d_pseudo[i] - mm(inverse[i], rate[i] * d_pseudo[i], ta=True) for i in heads]
    d_keys = [mm(d_scores[i], units[i], ta=True) for i in heads]
    done = [unit_grad(invs[i], units[i], d_units[i]) for i in heads]
    for i in heads:
        o.err[i] = errs[i]
        o.dk[i] = d_keys[i]
        o.z[i] = z[i]
        store_strided(of, me ^ i, gain * normal[i])
        store_strided(df, me ^ i, done[i])
    o.normed[...] = of[...].astype(BF16)
    o.dq[...] = df[...].astype(BF16)


def gain_kernel(n, o):
    o.gain[...] = sum(ref[HALF : HALF + 1, :] for ref in n.states + n.adjoints)


def last_kernel(group, n, o, df, vf):
    me = place_in(group)
    rates = n.rates[...]
    steps, count = rates.shape
    heads = range(count)
    rate = [rate_column(rates, me ^ i) for i in heads]
    raws = [strided(n.kf, me ^ i, steps) for i in heads]
    adjoints = [ref[:HALF, :] for ref in n.adjoints]
    states = [ref[:HALF, :] for ref in n.states]
    units = take(n.unit, heads)
    errs, kx, z0, dk0 = ([x[i] for i in heads] for x in (n.err, n.kx, n.z, n.dk))
    z = [z0[i] + mm(kx[i], adjoints[i]) for i in heads]
    invs = [inverse_norm(raw) for raw in raws]
    pseudo = [rate[i] * errs[i] for i in heads]
    d_values = [rate[i] * z[i] for i in heads]
    half = steps // 2
    below = iota((half, half), 1) < iota((half, half), 0)
    d_grams = []
    for i in heads:
        later = mm(d_values[i][half:], pseudo[i], tb=True)
        corners = [
            jnp.where(below, corner, 0.0)
            for corner in (mm(d_values[i][:half], pseudo[i][:half], tb=True), later[:, half:])
        ]
        corners = [corner + corner.T for corner in corners]
        d_grams.append(
            jnp.concatenate(
                [
                    jnp.concatenate([corners[0], later[:, :half].T], axis=1),
                    jnp.concatenate([later[:, :half], corners[1]], axis=1),
                ],
                axis=0,
            )
        )
    d_units = [
        dk0[i]
        + mm(
            jnp.concatenate([pseudo[i], d_values[i], d_grams[i]], axis=1),
            jnp.concatenate([adjoints[i].T, -states[i].T, -units[i]], axis=0),
        )
        for i in heads
    ]
    done = [unit_grad(invs[i], units[i], d_units[i]) for i in heads]
    d_rates = jnp.zeros(rates.shape, F32)
    for i in heads:
        d_rate = jnp.sum(z[i] * errs[i], axis=1, keepdims=True)
        d_rates = jnp.where(iota(rates.shape, 1) == me ^ i, d_rate, d_rates)
        store_strided(vf, me ^ i, d_values[i])
        store_strided(df, me ^ i, done[i])
    o.dk[...] = df[...].astype(BF16)
    o.dv[...] = vf[...].astype(BF16)
    for j in range(2):
        o.db[j * count : (j + 1) * count, :] = pick(d_rates, places(steps, j), ta=True)


def f32(*shape):
    return pltpu.VMEM(shape, F32)


def out(dtype, *shape):
    return jax.ShapeDtypeStruct(shape, dtype)


def call(body, ins, outs, scratch=(), hbm=(), after=(), flops=1000, shared={}):
    names = [name for name in ins]
    flat, tree = jax.tree.flatten([ins[name] for name in names])
    outs = dict(outs)
    flat_outs, out_tree = jax.tree.flatten(outs)
    specs = jax.tree.leaves(
        [
            jax.tree.map(
                lambda _: pl.BlockSpec(memory_space=pltpu.HBM if name in hbm else pltpu.VMEM),
                ins[name],
            )
            for name in names
        ]
    )
    after = list(after)

    def kernel(*refs):
        values = jax.tree.unflatten(tree, refs[: len(flat)])
        start = len(flat) + len(after)
        results = jax.tree.unflatten(out_tree, refs[start : start + len(flat_outs)])
        results.update({name: results[old] for name, old in shared.items()})
        body(
            types.SimpleNamespace(**dict(zip(names, values))),
            types.SimpleNamespace(**results),
            *refs[start + len(flat_outs) :],
        )

    results = pl.pallas_call(
        kernel,
        out_shape=flat_outs,
        in_specs=specs + [pl.BlockSpec(memory_space=pl.ANY)] * len(after),
        scratch_shapes=[pltpu.VMEM(s, F32) if isinstance(s, tuple) else s for s in scratch],
        compiler_params=pltpu.CompilerParams(vmem_limit_bytes=16 * 1024 * 1024),
        cost_estimate=pl.CostEstimate(flops=flops, bytes_accessed=0, transcendentals=0),
    )(*flat, *after)
    return types.SimpleNamespace(**jax.tree.unflatten(out_tree, results))


def swap(piece, i):
    return lax.ppermute(piece, "seq", [(d, d ^ i) for d in range(lax.axis_size("seq"))])


def local(queries, keys, values, betas, gain, out_grad):
    tokens, heads, dim = queries.shape
    substeps = keys.shape[1]
    steps = tokens * substeps
    group = GROUP
    count = lax.axis_size("seq")
    groups = count // group
    two = groups == 2
    bind = functools.partial
    q2 = queries.reshape(tokens * heads, dim)
    g2 = out_grad.reshape(tokens * heads, dim)
    k2 = keys.reshape(steps * heads, dim)
    v2 = values.reshape(steps * heads, dim)
    packed = betas.transpose(1, 2, 0).reshape(substeps * heads, tokens)

    def chunk_outs(*widths):
        return dict(
            maps=[f32(dim, width) for width in widths],
            unit=f32(2, steps, dim),
            inverse=f32(2, steps, steps),
            w=f32(2, steps, dim),
            e=f32(2, steps, dim),
        )

    read_outs = dict(q_unit=f32(2, tokens, dim), scores=f32(2, tokens, steps))
    a = call(
        bind(first_kernel, group, SOONER),
        {
            name: pltpu.with_memory_space_constraint(x, pltpu.HBM)
            for name, x in (
                ("k", k2),
                ("v", v2),
                ("q", q2),
                ("og", g2),
                ("packed", packed),
                ("gain", gain.reshape(1, dim)),
            )
        },
        dict(
            chunk_outs(5 * dim, 2 * dim),
            **read_outs,
            later_reads=f32(tokens, 3 * dim),
            rates=f32(steps, heads),
            rows=f32(heads, steps),
            kf=f32(steps * heads, dim),
            vf=f32(steps * heads, dim),
            qf=f32(tokens * heads, dim),
            gf=f32(tokens * heads, dim),
            gain=f32(1, dim),
        ),
        scratch=[pltpu.VMEM((steps * heads, dim), BF16)] * 2
        + [pltpu.VMEM((tokens * heads, dim), BF16)] * 2
        + [(substeps * heads, tokens), pltpu.SemaphoreType.DMA((6,))],
        hbm=("k", "v", "q", "og", "packed", "gain"),
    )
    got = {h: swap(a.maps[i], h) for i, h in enumerate(SOONER)}
    b = call(
        bind(next_kernel, group, LATER),
        dict(kf=a.kf, vf=a.vf, rates=a.rates, rows=a.rows),
        chunk_outs(2 * dim, 2 * dim),
    )
    for i, h in enumerate(LATER):
        got[h] = swap(b.maps[i], h) if h else b.maps[i]
    unit, inverse, w, e = (
        [getattr(x, name) for x in (a, b)] for name in ("unit", "inverse", "w", "e")
    )
    rates = a.rates
    c = call(
        bind(second_kernel, group, LATER),
        dict(qf=a.qf, gf=a.gf, rates=rates, unit=unit, inverse=inverse, w=w, e=e),
        dict(read_outs, reads=[f32(tokens, 3 * dim)] * 2, kx=f32(heads, steps, dim)),
        after=[got[SOONER[1]]],
        flops=10**9,
    )
    q_unit, scores = [a.q_unit, c.q_unit], [a.scores, c.scores]
    one = call(hold_kernel, dict(x=a.later_reads), dict(y=f32(tokens, 3 * dim)), after=[b.unit]).y
    own_reads = dict(zip(SOONER + LATER, [a.maps[0], one] + c.reads))
    got_reads = dict(own_reads)
    got_reads[SOONER[0]] = got[SOONER[0]]
    got_reads[SOONER[1]] = swap(one, SOONER[1])
    held = call(
        hold_kernel, dict(x=c.reads[0]), dict(y=f32(tokens, 3 * dim)), after=[got[SOONER[0]]]
    ).y
    got_reads[LATER[0]] = swap(held, LATER[0])
    own_reads, got_reads = ([x[h] for h in range(heads)] for x in (own_reads, got_reads))
    j = call(
        bind(join_kernel, group),
        dict(maps=[got[h] for h in range(heads)]),
        dict(
            starts=f32(group, dim, dim), total=f32(dim, dim), maps=f32(group, dim, 2 * dim)
        ),
        after=[c.kx],
    )
    ahead = [(d, d + group) for d in range(count - group)]
    behind = [(d + group, d) for d in range(count - group)]
    across = [(d, d ^ group) for d in range(count)]
    entry = lax.ppermute(j.total, "seq", across if two else ahead)
    p = call(
        bind(products_kernel, group),
        dict(maps=j.maps),
        dict(
            before=f32(group + 1, dim, dim),
            after=f32(group, dim, dim),
            middle=f32(dim, dim),
        ),
    )
    for _ in range(groups - 2):
        passed = jnp.dot(p.before[group], entry, precision=lax.Precision.HIGHEST) + j.total
        entry = lax.ppermute(passed, "seq", ahead)
    own = call(
        bind(owner_kernel, group, 1 if two else None),
        dict(
            entry=entry,
            reads=got_reads,
            gain=a.gain,
            maps=j.maps,
            before=p.before,
            middle=p.middle,
            starts=j.starts,
        ),
        dict(
            starts=f32(group, dim, dim),
            entries=f32(group, dim, dim),
            total=f32(dim + 8, dim),
            states=[f32(dim + 8, dim)] * heads,
        ),
        scratch=[(group, tokens, 3 * dim)],
    )
    entry = lax.ppermute(own.total, "seq", across if two else behind)
    for _ in range(groups - 2):
        passed = jnp.dot(p.before[group].T, entry[:dim], precision=lax.Precision.HIGHEST)
        entry = lax.ppermute(own.total.at[:dim].add(passed), "seq", behind)
    states = [own.states[0]] + [swap(own.states[h], h) for h in range(1, heads)]
    adjoints = call(
        bind(spread_kernel, group, 0 if two else None),
        dict(entry=entry, starts=own.starts, maps=p.after),
        dict(adjoints=[f32(dim + 8, dim)] * heads),
    ).adjoints
    first_adjoint = adjoints[0]
    adjoints = [adjoints[0]] + [swap(adjoints[h], h) for h in range(1, heads)]
    t = call(
        bind(tokens_kernel, group),
        dict(
            states=states,
            reads=own_reads,
            gain=a.gain,
            qf=a.qf,
            rates=rates,
            w=w,
            e=e,
            q_unit=q_unit,
            unit=unit,
            scores=scores,
            inverse=inverse,
        ),
        dict(
            normed=out(BF16, tokens * heads, dim),
            dq=out(BF16, tokens * heads, dim),
            err=f32(heads, steps, dim),
            dk=f32(heads, steps, dim),
            z=f32(heads, steps, dim),
        ),
        scratch=[(tokens * heads, dim)] * 2,
        after=[first_adjoint],
    )
    sums = call(
        gain_kernel, dict(states=states, adjoints=adjoints), dict(gain=f32(1, dim)), after=[t.err]
    ).gain
    size = lax.axis_size("head")
    last = call(
        bind(last_kernel, group),
        dict(
            kf=a.kf,
            rates=rates,
            unit=unit,
            err=t.err,
            kx=c.kx,
            z=t.z,
            dk=t.dk,
            adjoints=adjoints,
            states=states,
        ),
        dict(
            dk=out(BF16, steps * heads, dim),
            dv=out(BF16, steps * heads, dim),
            db=out(F32, substeps * heads, tokens),
        ),
        scratch=[(steps * heads, dim)] * 2,
        after=[sums],
    )
    if two:
        gain_sum = sums + sum(
            lax.ppermute(sums, "head", [(d, d ^ flip) for d in range(size)])
            for flip in range(1, size)
        )
    else:
        gain_sum = lax.psum(own.total[dim:][:1], ("seq", "head"))
    return (
        t.normed.reshape(tokens, heads, dim),
        t.dq.reshape(tokens, heads, dim),
        last.dk.reshape(tokens, substeps, heads, dim),
        last.dv.reshape(tokens, substeps, heads, dim),
        last.db.reshape(substeps, heads, tokens).transpose(2, 0, 1),
        gain_sum.reshape(dim),
    )


def solution(mesh):
    return jax.shard_map(
        local,
        mesh=mesh,
        in_specs=(
            P("seq", "head", None),
            P("seq", None, "head", None),
            P("seq", None, "head", None),
            P("seq", None, "head"),
            P(),
            P("seq", "head", None),
        ),
        out_specs=(
            P("seq", "head", None),
            P("seq", "head", None),
            P("seq", None, "head", None),
            P("seq", None, "head", None),
            P("seq", None, "head"),
            P(),
        ),
        check_vma=False,
    )
```

```python
import functools
import types

import jax
import jax.numpy as jnp
from jax import lax
from jax.experimental import pallas as pl
from jax.experimental.pallas import tpu as pltpu
from jax.sharding import PartitionSpec as P

EPS = 1e-06
GROUP = 4
HALF = 128
BASE = 16
F32 = jnp.float32
BF16 = jnp.bfloat16


def split(x):
    high = x.astype(BF16)
    return high, (x - high.astype(F32)).astype(BF16)


def mm(a, b, ta=False, tb=False):
    (ah, al), (bh, bl) = split(a), split(b)
    if ta:
        ah, al = ah.T, al.T
    dims = (((1,), (1 if tb else 0,)), ((), ()))
    if b.shape[0 if tb else 1] > 128:
        left = jnp.concatenate([ah, ah, al], axis=1)
        right = jnp.concatenate([bh, bl, bh], axis=1 if tb else 0)
        return lax.dot_general(left, right, dims, preferred_element_type=F32)
    left = jnp.concatenate([ah, al], axis=1)
    if tb:
        right = jnp.concatenate(
            [jnp.concatenate([bh, bh], axis=1), jnp.concatenate([bl, bl], axis=1)], axis=0
        )
        width = b.shape[0]
    else:
        right = jnp.concatenate([bh, bl], axis=1)
        right = jnp.concatenate([right, right], axis=0)
        width = b.shape[1]
    both = lax.dot_general(left, right, dims, preferred_element_type=F32)
    return both[:, :width] + both[:, width:]


def exact_nt(a, b):
    return lax.dot_general(a, b, (((1,), (1,)), ((), ())), preferred_element_type=F32)


def iota(shape, dim):
    return lax.broadcasted_iota(jnp.int32, shape, dim)


def row_of(column):
    square = jnp.where(iota((HALF, HALF), 0) == iota((HALF, HALF), 1), column, 0.0)
    return jnp.sum(square, axis=0, keepdims=True)


def places(steps, j):
    shape = (steps, steps // 2)
    return (iota(shape, 0) == 2 * iota(shape, 1) + j).astype(F32)


def pick(a, b, ta=False, tb=False):
    dims = (((0 if ta else 1,), (1 if tb else 0,)), ((), ()))
    return lax.dot_general(
        a, b, dims, precision=lax.Precision.HIGHEST, preferred_element_type=F32
    )


def rate_column(rates, head):
    return jnp.sum(jnp.where(iota(rates.shape, 1) == head, rates, 0.0), axis=1, keepdims=True)


def small_inverses(lowers, rate_rows):
    blocks = HALF // BASE
    lane = iota((BASE, HALF), 1)
    row = iota((BASE, HALF), 0)
    jobs = range(len(lowers))
    packed = []
    for lower in lowers:
        one = lower[:BASE]
        for b in range(1, blocks):
            one = jnp.where(lane // BASE == b, lower[b * BASE : (b + 1) * BASE], one)
        packed.append(one)
    scaled = [packed[n] * rate_rows[n] for n in jobs]
    for j in range(BASE - 1):
        index = lane // BASE * BASE + j
        factors = [
            jnp.take_along_axis(scaled[n], index, axis=1, mode="promise_in_bounds") for n in jobs
        ]
        packed = [
            packed[n] - jnp.where(row > j, factors[n], 0.0) * packed[n][j : j + 1] for n in jobs
        ]
    return [
        jnp.concatenate(
            [jnp.where(lane // BASE == b, one, 0.0) for b in range(blocks)], axis=0
        )
        for one in packed
    ]


def place_in(group):
    return lax.rem(lax.axis_index("seq"), group)


def strided(ref, head, rows):
    return ref[pl.ds(head, rows, stride=ref.shape[0] // rows), :]


def store_strided(ref, head, value):
    rows = value.shape[0]
    ref[pl.ds(head, rows, stride=ref.shape[0] // rows), :] = value


SOONER, LATER = (2, 1), (3, 0)


def take(pairs, heads):
    order = SOONER + LATER
    return [pairs[order.index(h) // 2][order.index(h) % 2] for h in heads]


def inverse_norm(rows):
    return lax.rsqrt(jnp.sum(rows * rows, axis=1, keepdims=True) + EPS)


def unit_grad(inv, unit, grad):
    return inv * (grad - unit * jnp.sum(unit * grad, axis=1, keepdims=True))


def chunk(me, heads, kf, vf, rates, rows, o, wait):
    steps = rates.shape[0]
    strict = iota((HALF, HALF), 1) < iota((HALF, HALF), 0)
    rate = [rate_column(rates, me ^ h) for h in heads]
    rate_rows = [rows[pl.ds(me ^ h, 1), :] for h in heads]
    sides = [slice(0, HALF), slice(HALF, 2 * HALF)]
    raws = [strided(kf, me ^ h, steps) for h in heads]
    heads = range(len(heads)) if wait is None else heads
    count = range(len(raws))
    invs = [inverse_norm(raw) for raw in raws]
    inv_rows = [[row_of(inv[side]) for side in sides] for inv in invs]
    units = [raw * inv for raw, inv in zip(raws, invs)]
    raw16 = [raw.astype(BF16) for raw in raws]
    jobs = [(i, b) for i in count for b in range(2)]
    diag = {
        (i, b): jnp.where(
            strict,
            exact_nt(raw16[i][sides[b]], raw16[i][sides[b]]) * invs[i][sides[b]] * inv_rows[i][b],
            0.0,
        )
        for i, b in jobs
    }
    cross = [
        exact_nt(raw16[i][sides[1]], raw16[i][sides[0]]) * invs[i][sides[1]] * inv_rows[i][0]
        for i in count
    ]
    across = {(i, b): rate_rows[i][:, sides[b]] for i, b in jobs}
    inverse = dict(zip(jobs, small_inverses([diag[n] for n in jobs], [across[n] for n in jobs])))
    size = BASE
    while size < HALF:
        r, c = iota((HALF, HALF), 0) // size, iota((HALF, HALF), 1) // size
        below = (r % 2 == 1) & (c == r - 1)
        part = {n: jnp.where(below, diag[n], 0.0) for n in jobs}
        right = {n: part[n] - mm(part[n] * across[n], inverse[n]) for n in jobs}
        inverse = {
            n: inverse[n] + right[n] - mm(inverse[n] * across[n], right[n]) for n in jobs
        }
        size *= 2
    right = [cross[i] - mm(cross[i] * across[i, 0], inverse[i, 0]) for i in count]
    joined = [right[i] - mm(inverse[i, 1] * across[i, 1], right[i]) for i in count]
    vals = vf()
    both = [jnp.concatenate([units[i], vals[i]], axis=1) for i in count]
    top = [both[i][:HALF] - mm(inverse[i, 0] * across[i, 0], both[i][:HALF]) for i in count]
    low = [
        jnp.concatenate([joined[i] * across[i, 0], inverse[i, 1] * across[i, 1]], axis=1)
        for i in count
    ]
    bottom = [both[i][HALF:] - mm(low[i], both[i]) for i in count]
    solved = [jnp.concatenate([top[i], bottom[i]], axis=0) for i in count]
    eye = (iota((HALF, 2 * HALF), 0) == iota((HALF, 2 * HALF), 1)).astype(F32)
    sign = jnp.where(iota((HALF, 2 * HALF), 1) < HALF, -1.0, 1.0)
    ends = [eye + sign * mm(units[i], rate[i] * solved[i], ta=True) for i in count]
    for i in count:
        o.maps[i][:, : 2 * HALF] = ends[i]
        o.unit[i] = units[i]
        o.inverse[i, :HALF, :HALF] = inverse[i, 0]
        o.inverse[i, :HALF, HALF:] = jnp.zeros((HALF, HALF), F32)
        o.inverse[i, HALF:, :HALF] = joined[i]
        o.inverse[i, HALF:, HALF:] = inverse[i, 1]
        o.w[i] = solved[i][:, :HALF]
        o.e[i] = solved[i][:, HALF:]
    return units, [x[:, :HALF] for x in solved], [x[:, HALF:] for x in solved]


def first_kernel(group, heads, n, o, k16, v16, q16, g16, p32, sems):
    copies = [
        pltpu.make_async_copy(src, dst, sems.at[c])
        for c, (src, dst) in enumerate(
            (
                (n.packed, p32),
                (n.k, k16),
                (n.v, v16),
                (n.q, q16),
                (n.og, g16),
                (n.gain, o.gain),
            )
        )
    ]
    for copy in copies:
        copy.start()
    me = place_in(group)
    steps, count = o.rates.shape
    copies[0].wait()
    packed = p32[...]
    own, place = [packed[:count], packed[count:]], [places(steps, j) for j in range(2)]
    rates = pick(place[0], own[0], tb=True) + pick(place[1], own[1], tb=True)
    o.rates[...] = rates
    o.rows[...] = pick(own[0], place[0], tb=True) + pick(own[1], place[1], tb=True)
    copies[1].wait()
    o.kf[...] = k16[...].astype(F32)
    copies[2].wait()
    o.vf[...] = v16[...].astype(F32)
    for copy in copies[3:]:
        copy.wait()
    o.qf[...] = q16[...].astype(F32)
    o.gf[...] = g16[...].astype(F32)
    tokens = steps // 2
    vals = [strided(o.vf, me ^ h, steps) for h in heads]
    qs = [strided(o.qf, me ^ h, tokens) for h in heads]
    given = [strided(o.gf, me ^ h, tokens) for h in heads]
    solved = chunk(me, heads, o.kf, lambda: vals, rates, o.rows, o, None)
    reads(heads, qs, given, rates, *solved, me, o, [o.maps[0], o.later_reads])


def next_kernel(group, heads, n, o):
    me = place_in(group)
    steps = n.rates.shape[0]
    vals = [strided(n.vf, me ^ h, steps) for h in heads]
    chunk(me, heads, n.kf, lambda: vals, n.rates[...], n.rows, o, None)


def reads(heads, qs, given, rates, keys, w, e, me, o, outs):
    tokens = qs[0].shape[0]
    steps = 2 * tokens
    count = range(len(heads))
    seen = iota((tokens, steps), 1) <= 2 * iota((tokens, steps), 0) + 1
    rate = [rate_column(rates, me ^ h) for h in heads]
    weighted = [rate[i] * jnp.concatenate([w[i], e[i]], axis=1) for i in count]
    units = [q * inverse_norm(q) for q in qs]
    scores = [jnp.where(seen, mm(units[i], keys[i], tb=True), 0.0) for i in count]
    rows = [mm(scores[i], weighted[i]) for i in count]
    for i in count:
        o.q_unit[i] = units[i]
        o.scores[i] = scores[i]
        out = outs[i]
        skip = out.shape[1] - 3 * HALF
        out[:, skip : skip + HALF] = units[i] - rows[i][:, :HALF]
        out[:, skip + HALF : skip + 2 * HALF] = rows[i][:, HALF:]
        out[:, skip + 2 * HALF :] = given[i]


def second_kernel(group, heads, n, o):
    me = place_in(group)
    tokens = o.scores.shape[1]
    rates = n.rates[...]
    qs = [strided(n.qf, me ^ h, tokens) for h in heads]
    given = [strided(n.gf, me ^ h, tokens) for h in heads]
    keys, w, e = (take(x, heads) for x in (n.unit, n.w, n.e))
    every = range(o.kx.shape[0])
    rate = [rate_column(rates, me ^ i) for i in every]
    units, inverse = (take(x, every) for x in (n.unit, n.inverse))
    spread = [units[i] - mm(inverse[i], rate[i] * units[i], ta=True) for i in every]
    reads(heads, qs, given, rates, keys, w, e, me, o, o.reads)
    for i in every:
        o.kx[i] = spread[i]


def hold_kernel(n, o):
    o.y[...] = n.x[...]


def join_kernel(group, n, o):
    me = place_in(group)
    for i, piece in enumerate(n.maps):
        o.maps[me ^ i] = piece[:, : 2 * HALF]
    state = jnp.zeros((HALF, HALF), F32)
    for j in range(group):
        o.starts[j] = state
        own = o.maps[j, :, HALF:]
        state = own if j == 0 else mm(o.maps[j, :, :HALF], state) + own
    o.total[...] = state


def products_kernel(group, n, o):
    eye = (iota((HALF, HALF), 0) == iota((HALF, HALF), 1)).astype(F32)
    steps = [n.maps[j, :, :HALF] for j in range(group)]
    before, after = [eye, steps[0]], [eye, steps[-1]]
    for j in range(1, group):
        before.append(mm(steps[j], before[-1]))
        after.append(mm(after[-1], steps[-1 - j]))
    o.middle[...] = mm(steps[2], steps[1])
    for j in range(group + 1):
        o.before[j] = before[j]
    for j in range(group):
        o.after[j] = after[group - 1 - j]


def spread_kernel(group, side, n, o):
    me = place_in(group)
    entry = n.entry[:HALF, :]
    if side is not None:
        entry = jnp.where(lax.axis_index("seq") // group == side, entry, 0.0)
    starts = [n.starts[me ^ i] for i in range(group)]
    maps = [n.maps[me ^ i] for i in range(group)]
    values = [starts[i] + mm(maps[i], entry, ta=True) for i in range(group)]
    for i, out in enumerate(o.adjoints):
        out[:HALF, :] = values[i]
        out[HALF:, :] = n.entry[HALF:, :]


def normed_and_grads(queries, parts, states, given, gain):
    count = range(len(queries))
    reads = [parts[i] + mm(queries[i], states[i]) for i in count]
    inv_rms = [lax.rsqrt(jnp.mean(read * read, axis=1, keepdims=True) + EPS) for read in reads]
    normal = [reads[i] * inv_rms[i] for i in count]
    scaled = [given[i] * gain for i in count]
    grads = [
        inv_rms[i] * (scaled[i] - normal[i] * jnp.mean(scaled[i] * normal[i], axis=1, keepdims=True))
        for i in count
    ]
    return normal, grads, sum(jnp.sum(given[i] * normal[i], axis=0, keepdims=True) for i in count)


def owner_kernel(group, side, n, o, packed):
    me = place_in(group)
    entry = n.entry[...]
    if side is not None:
        entry = jnp.where(lax.axis_index("seq") // group == side, entry, 0.0)
    for i, piece in enumerate(n.reads):
        packed[me ^ i] = piece[:, piece.shape[1] - 3 * HALF :]
    gain = n.gain[...]
    places_ = range(group)
    maps = [n.maps[j, :, :HALF] for j in places_]
    before = [n.before[j] for j in places_]
    starts = [n.starts[j] for j in places_]
    queries, parts, given = (
        [packed[j, :, c * HALF : (c + 1) * HALF] for j in places_] for c in range(3)
    )
    states = [starts[j] + mm(before[j], entry) if j else starts[j] + entry for j in places_]
    _, grads, gain_part = normed_and_grads(queries, parts, states, given, gain)
    adjoints = [mm(queries[j], grads[j], ta=True) for j in places_]
    chain = [
        adjoints[1] + mm(maps[1], adjoints[2], ta=True) + mm(n.middle[...], adjoints[3], ta=True),
        adjoints[2] + mm(maps[2], adjoints[3], ta=True),
        adjoints[3],
        jnp.zeros((HALF, HALF), F32),
    ]
    total = adjoints[0] + sum(mm(before[j], adjoints[j], ta=True) for j in range(1, group))
    for j in places_:
        o.starts[j] = chain[j]
        o.entries[j] = states[j]
    o.total[:HALF, :] = total
    for i in places_:
        o.states[i][:HALF, :] = o.entries[me ^ i]
        o.states[i][HALF:, :] = jnp.broadcast_to(gain_part, (8, HALF))
    o.total[HALF:, :] = jnp.broadcast_to(gain_part, (8, HALF))


def tokens_kernel(group, n, o, of, df):
    me = place_in(group)
    heads, tokens, steps = range(len(n.reads)), n.reads[0].shape[0], n.rates.shape[0]
    gain = n.gain[...]
    rates = n.rates[...]
    queries, parts, given = (
        [
            ref[:, ref.shape[1] - (3 - c) * HALF : ref.shape[1] - (2 - c) * HALF]
            for ref in n.reads
        ]
        for c in range(3)
    )
    states = [ref[:HALF, :] for ref in n.states]
    seen = iota((tokens, steps), 1) <= 2 * iota((tokens, steps), 0) + 1
    raws = [strided(n.qf, me ^ i, tokens) for i in heads]
    keys, w, e, units, inverse, scores = (
        take(x, heads) for x in (n.unit, n.w, n.e, n.q_unit, n.inverse, n.scores)
    )
    rate = [rate_column(rates, me ^ i) for i in heads]
    invs = [inverse_norm(raw) for raw in raws]
    errs = [e[i] - mm(w[i], states[i]) for i in heads]
    normal, grads, _ = normed_and_grads(queries, parts, states, given, gain)
    pseudo = [rate[i] * errs[i] for i in heads]
    d_scores = [jnp.where(seen, mm(grads[i], pseudo[i], tb=True), 0.0) for i in heads]
    d_pseudo = [mm(scores[i], grads[i], ta=True) for i in heads]
    d_units = [mm(grads[i], states[i], tb=True) + mm(d_scores[i], keys[i]) for i in heads]
    z = [d_pseudo[i] - mm(inverse[i], rate[i] * d_pseudo[i], ta=True) for i in heads]
    d_keys = [mm(d_scores[i], units[i], ta=True) for i in heads]
    done = [unit_grad(invs[i], units[i], d_units[i]) for i in heads]
    for i in heads:
        o.err[i] = errs[i]
        o.dk[i] = d_keys[i]
        o.z[i] = z[i]
        store_strided(of, me ^ i, gain * normal[i])
        store_strided(df, me ^ i, done[i])
    o.normed[...] = of[...].astype(BF16)
    o.dq[...] = df[...].astype(BF16)


def gain_kernel(n, o):
    o.gain[...] = sum(ref[HALF : HALF + 1, :] for ref in n.states + n.adjoints)


def last_kernel(group, n, o, df, vf):
    me = place_in(group)
    rates = n.rates[...]
    steps, count = rates.shape
    heads = range(count)
    rate = [rate_column(rates, me ^ i) for i in heads]
    raws = [strided(n.kf, me ^ i, steps) for i in heads]
    adjoints = [ref[:HALF, :] for ref in n.adjoints]
    states = [ref[:HALF, :] for ref in n.states]
    units = take(n.unit, heads)
    errs, kx, z0, dk0 = ([x[i] for i in heads] for x in (n.err, n.kx, n.z, n.dk))
    z = [z0[i] + mm(kx[i], adjoints[i]) for i in heads]
    invs = [inverse_norm(raw) for raw in raws]
    pseudo = [rate[i] * errs[i] for i in heads]
    d_values = [rate[i] * z[i] for i in heads]
    half = steps // 2
    below = iota((half, half), 1) < iota((half, half), 0)
    d_grams = []
    for i in heads:
        later = mm(d_values[i][half:], pseudo[i], tb=True)
        corners = [
            jnp.where(below, corner, 0.0)
            for corner in (mm(d_values[i][:half], pseudo[i][:half], tb=True), later[:, half:])
        ]
        corners = [corner + corner.T for corner in corners]
        d_grams.append(
            jnp.concatenate(
                [
                    jnp.concatenate([corners[0], later[:, :half].T], axis=1),
                    jnp.concatenate([later[:, :half], corners[1]], axis=1),
                ],
                axis=0,
            )
        )
    d_units = [
        dk0[i]
        + mm(
            jnp.concatenate([pseudo[i], d_values[i], d_grams[i]], axis=1),
            jnp.concatenate([adjoints[i].T, -states[i].T, -units[i]], axis=0),
        )
        for i in heads
    ]
    done = [unit_grad(invs[i], units[i], d_units[i]) for i in heads]
    d_rates = jnp.zeros(rates.shape, F32)
    for i in heads:
        d_rate = jnp.sum(z[i] * errs[i], axis=1, keepdims=True)
        d_rates = jnp.where(iota(rates.shape, 1) == me ^ i, d_rate, d_rates)
        store_strided(vf, me ^ i, d_values[i])
        store_strided(df, me ^ i, done[i])
    o.dk[...] = df[...].astype(BF16)
    o.dv[...] = vf[...].astype(BF16)
    for j in range(2):
        o.db[j * count : (j + 1) * count, :] = pick(d_rates, places(steps, j), ta=True)


def f32(*shape):
    return pltpu.VMEM(shape, F32)


def out(dtype, *shape):
    return jax.ShapeDtypeStruct(shape, dtype)


def call(body, ins, outs, scratch=(), hbm=(), after=(), flops=1000, shared={}):
    names = [name for name in ins]
    flat, tree = jax.tree.flatten([ins[name] for name in names])
    outs = dict(outs)
    flat_outs, out_tree = jax.tree.flatten(outs)
    specs = jax.tree.leaves(
        [
            jax.tree.map(
                lambda _: pl.BlockSpec(memory_space=pltpu.HBM if name in hbm else pltpu.VMEM),
                ins[name],
            )
            for name in names
        ]
    )
    after = list(after)

    def kernel(*refs):
        values = jax.tree.unflatten(tree, refs[: len(flat)])
        start = len(flat) + len(after)
        results = jax.tree.unflatten(out_tree, refs[start : start + len(flat_outs)])
        results.update({name: results[old] for name, old in shared.items()})
        body(
            types.SimpleNamespace(**dict(zip(names, values))),
            types.SimpleNamespace(**results),
            *refs[start + len(flat_outs) :],
        )

    results = pl.pallas_call(
        kernel,
        out_shape=flat_outs,
        in_specs=specs + [pl.BlockSpec(memory_space=pl.ANY)] * len(after),
        scratch_shapes=[pltpu.VMEM(s, F32) if isinstance(s, tuple) else s for s in scratch],
        compiler_params=pltpu.CompilerParams(vmem_limit_bytes=16 * 1024 * 1024),
        cost_estimate=pl.CostEstimate(flops=flops, bytes_accessed=0, transcendentals=0),
    )(*flat, *after)
    return types.SimpleNamespace(**jax.tree.unflatten(out_tree, results))


def swap(piece, i):
    return lax.ppermute(piece, "seq", [(d, d ^ i) for d in range(lax.axis_size("seq"))])


def local(queries, keys, values, betas, gain, out_grad):
    tokens, heads, dim = queries.shape
    substeps = keys.shape[1]
    steps = tokens * substeps
    group = GROUP
    count = lax.axis_size("seq")
    groups = count // group
    two = groups == 2
    bind = functools.partial
    q2 = queries.reshape(tokens * heads, dim)
    g2 = out_grad.reshape(tokens * heads, dim)
    k2 = keys.reshape(steps * heads, dim)
    v2 = values.reshape(steps * heads, dim)
    packed = betas.transpose(1, 2, 0).reshape(substeps * heads, tokens)

    def chunk_outs(*widths):
        return dict(
            maps=[f32(dim, width) for width in widths],
            unit=f32(2, steps, dim),
            inverse=f32(2, steps, steps),
            w=f32(2, steps, dim),
            e=f32(2, steps, dim),
        )

    read_outs = dict(q_unit=f32(2, tokens, dim), scores=f32(2, tokens, steps))
    a = call(
        bind(first_kernel, group, SOONER),
        {
            name: pltpu.with_memory_space_constraint(x, pltpu.HBM)
            for name, x in (
                ("k", k2),
                ("v", v2),
                ("q", q2),
                ("og", g2),
                ("packed", packed),
                ("gain", gain.reshape(1, dim)),
            )
        },
        dict(
            chunk_outs(5 * dim, 2 * dim),
            **read_outs,
            later_reads=f32(tokens, 3 * dim),
            rates=f32(steps, heads),
            rows=f32(heads, steps),
            kf=f32(steps * heads, dim),
            vf=f32(steps * heads, dim),
            qf=f32(tokens * heads, dim),
            gf=f32(tokens * heads, dim),
            gain=f32(1, dim),
        ),
        scratch=[pltpu.VMEM((steps * heads, dim), BF16)] * 2
        + [pltpu.VMEM((tokens * heads, dim), BF16)] * 2
        + [(substeps * heads, tokens), pltpu.SemaphoreType.DMA((6,))],
        hbm=("k", "v", "q", "og", "packed", "gain"),
    )
    got = {h: swap(a.maps[i], h) for i, h in enumerate(SOONER)}
    b = call(
        bind(next_kernel, group, LATER),
        dict(kf=a.kf, vf=a.vf, rates=a.rates, rows=a.rows),
        chunk_outs(2 * dim, 2 * dim),
    )
    for i, h in enumerate(LATER):
        got[h] = swap(b.maps[i], h) if h else b.maps[i]
    unit, inverse, w, e = (
        [getattr(x, name) for x in (a, b)] for name in ("unit", "inverse", "w", "e")
    )
    rates = a.rates
    c = call(
        bind(second_kernel, group, LATER),
        dict(qf=a.qf, gf=a.gf, rates=rates, unit=unit, inverse=inverse, w=w, e=e),
        dict(read_outs, reads=[f32(tokens, 3 * dim)] * 2, kx=f32(heads, steps, dim)),
        after=[got[SOONER[1]]],
        flops=10**9,
    )
    q_unit, scores = [a.q_unit, c.q_unit], [a.scores, c.scores]
    one = call(hold_kernel, dict(x=a.later_reads), dict(y=f32(tokens, 3 * dim)), after=[b.unit]).y
    own_reads = dict(zip(SOONER + LATER, [a.maps[0], one] + c.reads))
    got_reads = dict(own_reads)
    got_reads[SOONER[0]] = got[SOONER[0]]
    got_reads[SOONER[1]] = swap(one, SOONER[1])
    held = call(
        hold_kernel, dict(x=c.reads[0]), dict(y=f32(tokens, 3 * dim)), after=[got[SOONER[0]]]
    ).y
    got_reads[LATER[0]] = swap(held, LATER[0])
    own_reads, got_reads = ([x[h] for h in range(heads)] for x in (own_reads, got_reads))
    j = call(
        bind(join_kernel, group),
        dict(maps=[got[h] for h in range(heads)]),
        dict(
            starts=f32(group, dim, dim), total=f32(dim, dim), maps=f32(group, dim, 2 * dim)
        ),
        after=[c.kx],
    )
    ahead = [(d, d + group) for d in range(count - group)]
    behind = [(d + group, d) for d in range(count - group)]
    across = [(d, d ^ group) for d in range(count)]
    entry = lax.ppermute(j.total, "seq", across if two else ahead)
    p = call(
        bind(products_kernel, group),
        dict(maps=j.maps),
        dict(
            before=f32(group + 1, dim, dim),
            after=f32(group, dim, dim),
            middle=f32(dim, dim),
        ),
    )
    for _ in range(groups - 2):
        passed = jnp.dot(p.before[group], entry, precision=lax.Precision.HIGHEST) + j.total
        entry = lax.ppermute(passed, "seq", ahead)
    own = call(
        bind(owner_kernel, group, 1 if two else None),
        dict(
            entry=entry,
            reads=got_reads,
            gain=a.gain,
            maps=j.maps,
            before=p.before,
            middle=p.middle,
            starts=j.starts,
        ),
        dict(
            starts=f32(group, dim, dim),
            entries=f32(group, dim, dim),
            total=f32(dim + 8, dim),
            states=[f32(dim + 8, dim)] * heads,
        ),
        scratch=[(group, tokens, 3 * dim)],
    )
    entry = lax.ppermute(own.total, "seq", across if two else behind)
    for _ in range(groups - 2):
        passed = jnp.dot(p.before[group].T, entry[:dim], precision=lax.Precision.HIGHEST)
        entry = lax.ppermute(own.total.at[:dim].add(passed), "seq", behind)
    states = [own.states[0]] + [swap(own.states[h], h) for h in range(1, heads)]
    adjoints = call(
        bind(spread_kernel, group, 0 if two else None),
        dict(entry=entry, starts=own.starts, maps=p.after),
        dict(adjoints=[f32(dim + 8, dim)] * heads),
    ).adjoints
    first_adjoint = adjoints[0]
    adjoints = [adjoints[0]] + [swap(adjoints[h], h) for h in range(1, heads)]
    t = call(
        bind(tokens_kernel, group),
        dict(
            states=states,
            reads=own_reads,
            gain=a.gain,
            qf=a.qf,
            rates=rates,
            w=w,
            e=e,
            q_unit=q_unit,
            unit=unit,
            scores=scores,
            inverse=inverse,
        ),
        dict(
            normed=out(BF16, tokens * heads, dim),
            dq=out(BF16, tokens * heads, dim),
            err=f32(heads, steps, dim),
            dk=f32(heads, steps, dim),
            z=f32(heads, steps, dim),
        ),
        scratch=[(tokens * heads, dim)] * 2,
        after=[first_adjoint, adjoints[1], adjoints[2]],
    )
    sums = call(
        gain_kernel, dict(states=states, adjoints=adjoints), dict(gain=f32(1, dim)), after=[t.err]
    ).gain
    size = lax.axis_size("head")
    last = call(
        bind(last_kernel, group),
        dict(
            kf=a.kf,
            rates=rates,
            unit=unit,
            err=t.err,
            kx=c.kx,
            z=t.z,
            dk=t.dk,
            adjoints=adjoints,
            states=states,
        ),
        dict(
            dk=out(BF16, steps * heads, dim),
            dv=out(BF16, steps * heads, dim),
            db=out(F32, substeps * heads, tokens),
        ),
        scratch=[(steps * heads, dim)] * 2,
        after=[sums],
    )
    if two:
        gain_sum = sums + sum(
            lax.ppermute(sums, "head", [(d, d ^ flip) for d in range(size)])
            for flip in range(1, size)
        )
    else:
        gain_sum = lax.psum(own.total[dim:][:1], ("seq", "head"))
    return (
        t.normed.reshape(tokens, heads, dim),
        t.dq.reshape(tokens, heads, dim),
        last.dk.reshape(tokens, substeps, heads, dim),
        last.dv.reshape(tokens, substeps, heads, dim),
        last.db.reshape(substeps, heads, tokens).transpose(2, 0, 1),
        gain_sum.reshape(dim),
    )


def solution(mesh):
    return jax.shard_map(
        local,
        mesh=mesh,
        in_specs=(
            P("seq", "head", None),
            P("seq", None, "head", None),
            P("seq", None, "head", None),
            P("seq", None, "head"),
            P(),
            P("seq", "head", None),
        ),
        out_specs=(
            P("seq", "head", None),
            P("seq", "head", None),
            P("seq", None, "head", None),
            P("seq", None, "head", None),
            P("seq", None, "head"),
            P(),
        ),
        check_vma=False,
    )
```
